128 devices in a mesh: row: 16 (over y, z), col: 8 (over x, core).
Axes of the slice: x: 4, y: 4, z: 4, core: 2. Of those that a mesh axis runs over, the one named last changes fastest.
Arguments:
- ancestor_inv: float32 [24576, 24576], P('row', 'col'), may hold values from -6 to 6
- update_tiles: int32 [96], replicated, may hold values from 0 to 191, as said below
- tile_slot: int32 [192], replicated, may hold values from 0 to 191, as said below
- lower_below: float32 [12288, 1024], P('col', 'row'), may hold values from -0.078125 to 0.078125
- diag_factor: float32 [1024, 1024], replicated
Outputs:
- cov_below: float32 [12288, 1024], P('row', 'col')
- cov_diag: float32 [1024, 1024], P(None, 'col')
The draws below stay inside these ranges and needn't reach their ends.
Inputs may be any that keep to these rules, and one draw needn't show every extreme that they name: `update_tiles`: strictly increasing; exactly 12 entries lie in each run of 24 ancestor tiles starting at a multiple of 24. `tile_slot`: A permutation; owner o holds slots 12 * o to 12 * o + 11. Of the update tiles 6 * i to 6 * i + 5, at most 1 have their slots with one owner, and exactly 1 with some owner.
All inputs are finite; a program needn't handle non-finite values.
Results may differ from the reference program's by a relative error of at most 0.000098.
Values sent between devices are 32-bit elements; how exact they have to be, the bound alone decides.
A program may use at most 192 MiB of HBM per device.

```python
import jax
import jax.numpy as jnp
from jax import lax

TILE = 128
ATILES = 192
UTILES = 96
JW = 1024
AORD = 24576
UPD = 12288
RT = 6
KT = 12
RS = 12
CB = 24
CAP = 1


def layout_tables(key):
    keys = jax.random.split(key, 5)
    col_blocks = ATILES // CB
    row_owners = ATILES // RS
    block_keys = jax.random.split(keys[0], col_blocks)
    picks = jax.vmap(lambda k: jnp.sort(jax.random.permutation(k, CB)[:KT]))(block_keys)
    update_list = (picks + (jnp.arange(col_blocks, dtype=jnp.int32) * CB)[:, None]).reshape(-1).astype(jnp.int32)
    sigma = jax.random.permutation(keys[1], row_owners).astype(jnp.int32)
    positions = jnp.arange(UTILES, dtype=jnp.int32)
    target = positions // RT
    within = positions % RT
    dest_keys = jax.random.split(keys[2], row_owners)
    group_perm = jax.vmap(lambda k: jax.random.permutation(k, RT))(dest_keys).astype(jnp.int32)
    group = group_perm[target, within] // CAP
    owner_update = sigma[(target + group) % row_owners]
    counts = jnp.sum((owner_update[:, None] == jnp.arange(row_owners, dtype=jnp.int32)[None, :]).astype(jnp.int32), axis=0)
    fill_owner = jnp.repeat(jnp.arange(row_owners, dtype=jnp.int32), RS - counts, total_repeat_length=ATILES - UTILES)
    marked = jnp.zeros((ATILES,), jnp.int32).at[update_list].set(1)
    owner_tile = jnp.zeros((ATILES,), jnp.int32).at[update_list].set(owner_update)
    random_order = jax.random.permutation(keys[3], ATILES).astype(jnp.int32)
    free_key = jnp.where(marked == 1, ATILES + random_order, random_order)
    free_tiles = jnp.argsort(free_key)[:ATILES - UTILES]
    owner_tile = owner_tile.at[free_tiles].set(fill_owner)
    tie_break = jax.random.permutation(keys[4], ATILES).astype(jnp.int32)
    slot_order = jnp.argsort(owner_tile * ATILES + tie_break)
    slots = jnp.zeros((ATILES,), jnp.int32).at[slot_order].set(jnp.arange(ATILES, dtype=jnp.int32))
    return (update_list, slots)


def draw_update_tiles(key, part):
    update_list, slots = layout_tables(key)
    return update_list


def draw_tile_slot(key, part):
    update_list, slots = layout_tables(key)
    return slots


def draw_diag_factor(key, part):
    key = jax.random.fold_in(key, 7)
    first, second = jax.random.split(key)
    diagonal = jax.random.uniform(first, (JW,), jnp.float32, 1.0, 2.0)
    below = jax.random.normal(second, (JW, JW), jnp.float32) * (0.35 / JW ** 0.5)
    return (jnp.tril(below, -1) + jnp.diag(diagonal)).astype(jnp.float32)


def spiked(values, stream_key, source, target, blocks, factor):
    owner, partner = [(jnp.arange(values.shape[axis_at]) // (values.shape[axis_at] // blocks)).reshape([-1 if axis == axis_at else 1 for axis in range(values.ndim)]) for axis_at in (source, target)]
    chosen = jax.random.permutation(stream_key, blocks)[partner]
    strong = (owner == chosen) | (owner == (partner + blocks // 2) % blocks)
    return jnp.where(strong, factor * values, values)


def levels(own_key, extent, pieces, smallest, largest):
    level, own = 1.0, jax.random.fold_in(own_key, 6)
    for axis_at, parts in pieces:
        heights = jnp.exp(jax.random.uniform(jax.random.fold_in(own, axis_at), (parts,), jnp.float32, smallest / len(pieces), largest / len(pieces)))
        level = level * jnp.repeat(heights, extent[axis_at] // parts).reshape([-1 if axis == axis_at else 1 for axis in range(len(extent))])
    return level


def gaussian(stream_key, dims, deviation, bound, pieces=(), held_as=jnp.bfloat16):
    gain = levels(stream_key, dims, pieces, -0.22, 0.18) if pieces else 1.0
    entries = jax.random.normal(stream_key, dims, jnp.float32) * deviation * gain
    return jnp.minimum(jnp.maximum(entries, -bound), bound).astype(held_as)


def noise_with(rng, dims, scale, limit, pieces, heavy, kind=jnp.bfloat16):
    entries = scale * jax.random.normal(rng, dims, jnp.float32)
    if pieces:
        entries = entries * levels(rng, dims, pieces, -0.22, 0.18)
    return jnp.clip(spiked(entries, jax.random.fold_in(rng, 3), *heavy), -limit, limit).astype(kind)


def setup_inputs(seed: int = 0) -> dict:
    seeds = jax.random.split(jax.random.key(seed), 6)
    return {
        "ancestor_inv": gaussian(seeds[0], (AORD, AORD), 1.0, 6.0, ((0, 16), (1, 8)), jnp.float32),
        "update_tiles": draw_update_tiles(jax.random.fold_in(seeds[5], 71), 0),
        "tile_slot": draw_tile_slot(jax.random.fold_in(seeds[5], 71), 0),
        "lower_below": noise_with(seeds[3], (UPD, JW), UPD ** -0.5, 0.078125, ((0, 8), (1, 16)), (0, 1, 16, 2.0), jnp.float32),
        "diag_factor": draw_diag_factor(jax.random.fold_in(seeds[5], 71), 0),
    }


def solve_right(rows, factor):
    return jax.scipy.linalg.solve_triangular(factor, rows.T, lower=True, trans=1).T

def reference(ancestor_inv, update_tiles, tile_slot, lower_below, diag_factor):
    offsets = jnp.arange(TILE, dtype=jnp.int32)
    row_index = (jnp.take(tile_slot, update_tiles)[:, None] * TILE + offsets[None, :]).reshape(-1).astype(jnp.int32)
    col_index = (update_tiles[:, None] * TILE + offsets[None, :]).reshape(-1).astype(jnp.int32)
    selected = jnp.take(jnp.take(ancestor_inv, row_index, axis=0), col_index, axis=1)
    scaled = solve_right(lower_below, diag_factor)
    cov_below = -jnp.dot(selected, scaled, precision=lax.Precision.HIGHEST)
    identity = jnp.eye(JW, dtype=jnp.float32)
    half_solve = jax.scipy.linalg.solve_triangular(diag_factor, identity, lower=True)
    diag_inverse = jax.scipy.linalg.solve_triangular(diag_factor, half_solve, lower=True, trans=1)
    cov_diag = diag_inverse - jnp.dot(scaled.T, cov_below, precision=lax.Precision.HIGHEST)
    return (cov_below, cov_diag)
```

```python
import jax
import jax.numpy as jnp
from jax import lax
from jax.experimental import pallas as pl
from jax.experimental.pallas import tpu as pltpu
from jax.sharding import PartitionSpec as P

TILE = 128
ATILES = 192
UTILES = 96
JW = 1024
MESH = pl.DeviceIdType.MESH
F32, BF16 = jnp.float32, jnp.bfloat16
VMEM = pl.BlockSpec(memory_space=pltpu.VMEM)
SMEM = pl.BlockSpec(memory_space=pltpu.SMEM)
ANY = pl.BlockSpec(memory_space=pl.ANY)
LIMIT = 60 * 1024 * 1024
ROWS, COLS, SLOT, FROM, OVER = 0, 8, 20, 36, 42


def spread(value, axis, root):
    mine = lax.axis_index(axis) == root
    return lax.psum(jnp.where(mine, value, jnp.zeros_like(value)), axis)


def solve_right(rows, factor):
    return jax.scipy.linalg.solve_triangular(factor, rows.T, lower=True, trans=1).T


def general(ancestor_inv, update_tiles, tile_slot, lower_below, diag_factor):
    rows_count = lax.axis_size("row")
    cols_count = lax.axis_size("col")
    this_row = lax.axis_index("row")
    this_col = lax.axis_index("col")
    share_rows = UTILES // rows_count
    share_cols = UTILES // cols_count
    slots_dev = ATILES // rows_count
    block_cols = ATILES // cols_count
    capacity = (share_rows + rows_count - 1) // rows_count
    narrow = JW // cols_count
    exact = lax.Precision.HIGHEST
    gathered = lax.all_gather(lower_below, "row", axis=1, tiled=True)
    scaled = solve_right(gathered, diag_factor)
    positions = jnp.arange(UTILES, dtype=jnp.int32)
    slot_of = jnp.take(tile_slot, update_tiles)
    owner_of = slot_of // slots_dev
    target_of = positions // share_rows
    same_group = (
        (owner_of[:, None] == owner_of[None, :])
        & (target_of[:, None] == target_of[None, :])
        & (positions[None, :] < positions[:, None])
    )
    rank_of = jnp.sum(same_group.astype(jnp.int32), axis=1)
    send_slots = jnp.arange(rows_count * capacity, dtype=jnp.int32)
    target_ids = send_slots // capacity
    rank_ids = send_slots % capacity
    matches = (
        (target_of[None, :] == target_ids[:, None])
        & (owner_of[None, :] == this_row)
        & (rank_of[None, :] == rank_ids[:, None])
    )
    local_slot = jnp.sum(jnp.where(matches, slot_of[None, :] - this_row * slots_dev, 0), axis=1)
    present = jnp.any(matches, axis=1).astype(jnp.float32)
    col_tiles = (
        lax.dynamic_slice_in_dim(update_tiles, this_col * share_cols, share_cols)
        - this_col * block_cols
    )
    tiled = ancestor_inv.reshape(slots_dev * TILE, block_cols, TILE)
    local_cols = jnp.take(tiled, col_tiles, axis=1).reshape(slots_dev, TILE, share_cols * TILE)
    own_positions = lax.dynamic_slice_in_dim(positions, this_row * share_rows, share_rows)
    arrival = jnp.take(owner_of, own_positions) * capacity + jnp.take(rank_of, own_positions)
    outgoing = jnp.take(local_cols, local_slot, axis=0) * present[:, None, None]
    incoming = lax.all_to_all(outgoing, "row", split_axis=0, concat_axis=0, tiled=True)
    front_tiles = jnp.take(incoming, arrival, axis=0).reshape(share_rows * TILE, share_cols * TILE)
    row_terms = jnp.dot(front_tiles, scaled, precision=exact)
    cov_below = -lax.psum_scatter(row_terms, "col", scatter_dimension=1, tiled=True)
    root = this_row * share_rows // share_cols
    start = this_row * share_rows % share_cols * TILE
    own_scaled = lax.dynamic_slice_in_dim(scaled, start, share_rows * TILE, 0)
    front_scaled = spread(own_scaled, "col", root)
    columns = (
        jnp.arange(JW, dtype=jnp.int32)[:, None]
        == this_col * narrow + jnp.arange(narrow, dtype=jnp.int32)[None, :]
    ).astype(jnp.float32)
    half_solve = jax.scipy.linalg.solve_triangular(diag_factor, columns, lower=True)
    diag_inverse = jax.scipy.linalg.solve_triangular(diag_factor, half_solve, lower=True, trans=1)
    cross = lax.psum(jnp.dot(front_scaled.T, cov_below, precision=exact), "row")
    cov_diag = diag_inverse - cross
    return (cov_below, cov_diag)


def split(value):
    high = value.astype(BF16)
    return high, (value - high.astype(F32)).astype(BF16)


def dot3(ah, al, bh, bl):
    out = jnp.dot(ah, bh, preferred_element_type=F32)
    out += jnp.dot(ah, bl, preferred_element_type=F32)
    return out + jnp.dot(al, bh, preferred_element_type=F32)


def exact(a, b):
    return jnp.dot(a, b, precision=lax.Precision.HIGHEST, preferred_element_type=F32)


def remote(src, dst, send, recv, row, col):
    return pltpu.make_async_remote_copy(
        src_ref=src, dst_ref=dst, send_sem=send, recv_sem=recv, device_id=(row, col), device_id_type=MESH
    )


def greet(peers):
    barrier = pltpu.get_barrier_semaphore()
    for peer in peers:
        pl.semaphore_signal(barrier, inc=1, device_id=peer, device_id_type=MESH)
    pl.semaphore_wait(barrier, len(peers))


def prepare(upd, slots, diag, lh, ll, th, tl, piece, table, inv, counts):
    row, col = lax.axis_index("row"), lax.axis_index("col")
    for i in range(64):
        table[i] = 0
    for i in range(16):
        counts[i] = 0

    def visit(u, carry):
        slot = slots[upd[u]]
        owner = slot // 12
        seen = counts[owner]
        counts[owner] = seen + 1

        @pl.when(seen >= 6)
        def _():
            table[OVER] = 1

        @pl.when((owner == row) & (seen < 6))
        def _():
            table[ROWS + seen] = slot - 12 * row
            table[SLOT + u // 6] = seen

        return carry

    lax.fori_loop(0, UTILES, visit, 0)
    for k in range(12):
        table[COLS + k] = upd[12 * col + k] - 24 * col
    for i in range(6):
        table[FROM + i] = slots[upd[6 * row + i]] // 12

    inv[...] = jnp.zeros_like(inv)
    i = lax.broadcasted_iota(jnp.int32, (256, 256), 0)
    j = lax.broadcasted_iota(jnp.int32, (256, 256), 1)
    for b in range(4):
        s = pl.ds(256 * b, 256)
        inv[s, s] = jnp.where(i == j, 1.0 / diag[s, s], 0.0)

    def level(n, carry):
        bi, bj = lax.shift_right_logical(i, n), lax.shift_right_logical(j, n)
        mask = (bi == bj + 1) & ((bi & 1) == 1)
        for b in range(4):
            s = pl.ds(256 * b, 256)
            x = inv[s, s]
            inv[s, s] = x - exact(x, exact(jnp.where(mask, diag[s, s], 0.0), x))
        return carry

    lax.fori_loop(0, 8, level, 0)
    for size in (256, 512):
        for b in range(512 // size):
            top, low = pl.ds(2 * size * b, size), pl.ds(2 * size * b + size, size)
            inv[low, top] = -exact(inv[low, low], exact(diag[low, top], inv[top, top]))

    def out(m, carry):
        s = pl.ds(pl.multiple_of(m * 128, 128), 128)
        x = inv[s, :]
        lh[s, :], ll[s, :] = split(x)
        th[:, s], tl[:, s] = split(x.T)
        return carry

    lax.fori_loop(0, 8, out, 0)
    piece[...] = inv[pl.ds(pl.multiple_of(row * 64, 64), 64), pl.ds(pl.multiple_of(col * 128, 128), 128)]


ITEMS = (
    (0, 0), (0, -1), (0, 1), (-1, 0), (1, 0), (0, 2), (-1, -1), (1, -1),
    (-1, 1), (1, 1), (2, 0), (-1, 2), (1, 2), (2, -1), (2, 1), (2, 2),
)


def front(
    table, anc, lb, lh, ll, cov_o, bro,
    ancv, bg, sh, sl, bh, bl, pa, pb, ph, pq, w, qr, qs, d2r, d1r, brx,
    anc_sem, gs, gr, xs, ps, sr, es, er, rs, rr, out_sem,
):
    row, col = lax.axis_index("row"), lax.axis_index("col")
    y, z, x, core = row // 4, row % 4, col // 2, col % 2
    other = 2 * x + 1 - core

    def at(dy, dz):
        return 4 * lax.rem(y + dy + 4, 4) + lax.rem(z + dz + 4, 4)

    def along(dx):
        return 2 * lax.rem(x + dx + 4, 4) + core

    loads = [
        pltpu.make_async_copy(anc.at[:, :, pl.ds(128 * t, 128)], ancv.at[t], anc_sem.at[t])
        for t in range(24)
    ]
    for load in loads:
        load.start()
    lane = lax.broadcasted_iota(jnp.int32, (128, 128), 1)
    for h in range(2):
        for m in range(3):
            low = lb[pl.ds(768 * h + 128 * m, 128), :]
            high = lb[pl.ds(768 * h + 384 + 128 * m, 128), :]
            bg[row, pl.ds(384 * h + 128 * m, 128), :] = jnp.concatenate([low, high], axis=1)
    greet(
        [(at(0, 1), col), (at(0, -1), col), (at(1, 0), col), (at(-1, 0), col)]
        + [(row, along(1)), (row, along(-1)), (row, other)]
    )

    def rel(h, a, b):
        return at(a, b) if h == 0 else at(b, a)

    ids = {}
    sends = []

    def gather(name, h, src, rows, step, recv_src):
        k = ids.setdefault((h, name), len(ids))
        part = pl.ds(384 * h + rows[0], rows[1])
        view = bg.at[rel(h, *src), part]
        copy = remote(view, view, gs.at[k], gr.at[k], rel(h, *step), col)
        copy.start()
        mine = bg.at[rel(h, *recv_src), part]
        got = remote(mine, mine, gs.at[k], gr.at[k], rel(h, *step), col)
        sends.append(copy)
        return got

    FULL, LOW, HIGH = (0, 384), (0, 192), (192, 192)
    arr = {}

    def first_phase(h):
        arr[h, 0, -1] = [gather("f+", h, (0, 0), FULL, (0, 1), (0, -1))]
        arr[h, 0, 1] = [gather("f-", h, (0, 0), FULL, (0, -1), (0, 1))]

    def first_forward(h):
        arr[h, 0, 2] = [
            gather("ff+", h, (0, -1), LOW, (0, 1), (0, -2)),
            gather("ff-", h, (0, 1), HIGH, (0, -1), (0, 2)),
        ]

    def second_phase(h, q):
        arr[h, -1, q] = [gather(("s+", q), h, (0, q), FULL, (1, 0), (-1, q))]
        arr[h, 1, q] = [gather(("s-", q), h, (0, q), FULL, (-1, 0), (1, q))]

    def second_forward(h, q):
        arr[h, 2, q] = [
            gather(("sf+", q), h, (-1, q), LOW, (1, 0), (-2, q)),
            gather(("sf-", q), h, (1, q), HIGH, (-1, 0), (2, q)),
        ]

    def wait(h, a, b):
        for got in arr[h, a, b]:
            got.wait_recv()

    parity = row % 2
    root_x, root_core = row // 4, (row // 2) % 2
    dist = lax.rem(x - root_x + 4, 4)
    ring = core == root_core
    S0, S1 = pl.ds(0, 192), pl.ds(192, 192)

    def piece_of(i):
        a, b = ITEMS[i]
        index = jnp.where(parity == 0, at(a, b), at(b, a))
        return index

    def spread_copies(i):
        def make(part, k, device):
            view = brx.at[i, part]
            return remote(view, view, xs.at[i, k], sr.at[i, k], row, device)

        def partner(part, k):
            view = brx.at[i, part]
            return remote(view, view, ps.at[i, k], sr.at[i, k], row, other)

        return make(S0, 0, along(1)), make(S1, 1, along(-1)), partner(S0, 0), partner(S1, 1)

    def spread_root(i):
        @pl.when(ring & (dist == 0))
        def _():
            brx[i] = bg[piece_of(i), pl.ds(pl.multiple_of(384 * parity, 384), 384), :]
            for copy in spread_copies(i):
                copy.start()

    def spread_hop(i, hop):
        up, down, pup, pdown = spread_copies(i)

        @pl.when(ring & (dist == hop))
        def _():
            up.wait_recv()
            if hop < 3:
                up.start()
            pup.start()

        @pl.when(ring & (dist == 4 - hop))
        def _():
            down.wait_recv()
            if hop < 3:
                down.start()
            pdown.start()

    def spread_end(i):
        up, down, pup, pdown = spread_copies(i)

        @pl.when(ring)
        def _():
            pup.wait_send()
            pdown.wait_send()

            @pl.when(dist != 3)
            def _():
                up.wait_send()

            @pl.when(dist != 1)
            def _():
                down.wait_send()

        @pl.when(jnp.logical_not(ring))
        def _():
            pup.wait_recv()
            pdown.wait_recv()

    def spread_step(i):
        if i < 16:
            spread_root(i)
        for hop in (1, 2, 3):
            if 0 <= i - hop < 16:
                spread_hop(i - hop, hop)

    def product(h, a):
        lead = lax.rem((y if h == 0 else z) + a + 4, 4)
        out = pa if h == 0 else pb
        for half in range(3):
            rows = pl.ds(384 * h + 128 * half, 128)
            low, high = pl.ds(128 * half, 128), pl.ds(384 + 128 * half, 128)
            for pair in range(2):
                if h == 0:
                    p0, p1 = bg[4 * lead + 2 * pair, rows, :], bg[4 * lead + 2 * pair + 1, rows, :]
                else:
                    p0, p1 = bg[4 * (2 * pair) + lead, rows, :], bg[4 * (2 * pair + 1) + lead, rows, :]
                cols = pl.ds(128 * pair, 128)
                bh[low, cols], bl[low, cols] = split(jnp.where(lane < 64, p0, pltpu.roll(p1, 64, 1)))
                bh[high, cols], bl[high, cols] = split(jnp.where(lane < 64, pltpu.roll(p0, 64, 1), p1))

        def body(m, carry):
            r = pl.ds(pl.multiple_of(m * 256, 256), 256)
            k = pl.ds(768 * h, 768)
            out[lead, r, :] = dot3(sh[r, k], sl[r, k], bh[...], bl[...])
            return carry

        lax.fori_loop(0, 3, body, 0)

    def extract(j, carry):
        dst = pl.ds(pl.multiple_of(j * 128, 128), 128)
        for k in range(12):
            tile = ancv[table[COLS + k], table[ROWS + j]]
            c = pl.ds(128 * k, 128)
            sh[dst, c], sl[dst, c] = split(tile)
        return carry

    both = (0, 1)
    for h in both:
        first_phase(h)
    for h in both:
        second_phase(h, 0)
    spread_step(0)
    for q in (-1, 1):
        for h in both:
            wait(h, 0, q)
        if q == 1:
            for h in both:
                first_forward(h)
        for h in both:
            second_phase(h, q)
    spread_step(1)
    spread_step(2)
    for h in both:
        wait(h, -1, 0)
        wait(h, 1, 0)
        second_forward(h, 0)
    spread_step(3)
    spread_step(4)
    for load in loads:
        load.wait()
    lax.fori_loop(0, 6, extract, 0)
    for h in both:
        wait(h, 0, 2)
        second_phase(h, 2)
    spread_step(5)
    product(0, 0)
    for q, i in ((-1, 6), (1, 8)):
        for h in both:
            wait(h, -1, q)
            wait(h, 1, q)
            second_forward(h, q)
        spread_step(i)
        spread_step(i + 1)
        if q == -1:
            product(1, 0)
    for h in both:
        wait(h, 2, 0)
    spread_step(10)
    for h in both:
        wait(h, -1, 2)
        wait(h, 1, 2)
        second_forward(h, 2)
    spread_step(11)
    spread_step(12)
    product(0, -1)
    product(1, -1)
    for h in both:
        wait(h, 2, -1)
        wait(h, 2, 1)
    spread_step(13)
    spread_step(14)
    product(0, 1)
    product(1, 1)
    for h in both:
        wait(h, 2, 2)
    spread_step(15)
    product(0, 2)
    product(1, 2)
    spread_step(16)

    def combine(m, carry):
        r = pl.ds(pl.multiple_of(m * 128, 128), 128)
        for yy in range(4):
            for pair in range(2):
                p0 = pb[2 * pair, r, pl.ds(128 * (yy // 2), 128)]
                p1 = pb[2 * pair + 1, r, pl.ds(128 * (yy // 2), 128)]
                if yy % 2 == 0:
                    mixed = jnp.where(lane < 64, p0, pltpu.roll(p1, 64, 1))
                else:
                    mixed = jnp.where(lane < 64, pltpu.roll(p0, 64, 1), p1)
                c = pl.ds(256 * yy + 128 * pair, 128)
                ph[r, c], pq[r, c] = split(pa[yy, r, pl.ds(128 * pair, 128)] + mixed)
        return carry

    lax.fori_loop(0, 6, combine, 0)
    spread_step(17)

    TOP, LOWER = pl.ds(0, 384), pl.ds(384, 384)
    swaps = []

    def columns(k, dx):
        c = pl.ds(pl.multiple_of(256 * lax.rem(x + dx + 4, 4), 256), 256)

        def body(m, carry):
            r = pl.ds(pl.multiple_of(m * 256, 256), 256)
            acc = dot3(ph[r, :], pq[r, :], lh[:, c], ll[:, c])
            w[0, k, r, :] = acc[:, :128]
            w[1, k, r, :] = acc[:, 128:]
            return carry

        lax.fori_loop(0, 3, body, 0)
        swap = remote(w.at[1 - core, k], qr.at[k], es.at[k], er.at[k], row, other)
        swap.start()
        swaps.append(swap)

    def merged(k):
        swaps[k].wait_recv()
        qs[k] = w[core, k] + qr[k]

    columns(0, 2)
    columns(1, 1)
    merged(0)
    up2 = remote(qs.at[0, TOP], d2r.at[0], rs.at[0], rr.at[0], row, along(1))
    down2 = remote(qs.at[0, LOWER], d2r.at[1], rs.at[1], rr.at[1], row, along(-1))
    up2.start()
    down2.start()
    columns(2, -1)
    merged(1)
    up_raw = remote(qs.at[1, LOWER], d1r.at[0, LOWER], rs.at[2], rr.at[2], row, along(1))
    up_raw.start()
    columns(3, 0)
    merged(2)
    down_raw = remote(qs.at[2, TOP], d1r.at[1, TOP], rs.at[3], rr.at[3], row, along(-1))
    down_raw.start()
    merged(3)
    spread_step(18)
    up2.wait_recv()
    qs[1, TOP] += d2r[0]
    up_sum = remote(qs.at[1, TOP], d1r.at[0, TOP], rs.at[4], rr.at[4], row, along(1))
    up_sum.start()
    down2.wait_recv()
    qs[2, LOWER] += d2r[1]
    down_sum = remote(qs.at[2, LOWER], d1r.at[1, LOWER], rs.at[5], rr.at[5], row, along(-1))
    down_sum.start()
    for i in range(16):
        spread_end(i)
    store = pltpu.make_async_copy(brx, bro, out_sem)
    store.start()
    for copy in sends:
        copy.wait_send()
    up_raw.wait_recv()
    down_raw.wait_recv()
    up_sum.wait_recv()
    down_sum.wait_recv()
    for t in range(6):
        r = pl.ds(128 * t, 128)
        cov_o[t] = -(qs[3, r] + d1r[0, r] + d1r[1, r])
    for copy in swaps + [up2, down2, up_raw, down_raw, up_sum, down_sum]:
        copy.wait_send()
    store.wait()


def back(
    table, cov_o, bro, th, tl, piece, cov, diag,
    slots, inc, brh, brl, wp, ws, wr, wall, ch, cl, as_, ar, bs, br, cs, cr,
):
    row, col = lax.axis_index("row"), lax.axis_index("col")
    y, z = row // 4, row % 4

    def at(dy, dz):
        return 4 * lax.rem(y + dy + 4, 4) + lax.rem(z + dz + 4, 4)

    peers = [lax.rem(row + d, 16) for d in range(1, 16)]
    origins = [lax.rem(row + 16 - d, 16) for d in range(1, 16)]
    greet([(peer, col) for peer in peers])
    for t in range(16):
        slots[t] = cov_o[table[SLOT + t]]
    tiles = []
    for k, peer in enumerate(peers):
        copy = remote(slots.at[peer], inc.at[row], as_.at[k], ar.at[k], peer, col)
        copy.start()
        tiles.append(copy)
    inc[row] = slots[row]
    parity = row % 2
    for i, (a, b) in enumerate(ITEMS):
        index = jnp.where(parity == 0, at(a, b), at(b, a))
        t = bro[i].T
        dst = pl.ds(pl.multiple_of(index * 64, 64), 64)
        brh[dst, pl.ds(0, 384)], brl[dst, pl.ds(0, 384)] = split(t[:64])
        brh[dst, pl.ds(384, 384)], brl[dst, pl.ds(384, 384)] = split(t[64:])
    for k, copy in enumerate(tiles):
        mine = inc.at[origins[k]]
        remote(mine, mine, as_.at[k], ar.at[k], peers[k], col).wait_recv()
    for i in range(6):
        tile = inc[table[FROM + i]]
        r = pl.ds(128 * i, 128)
        cov[r, :] = tile
        ch[r, :], cl[r, :] = split(tile)

    def cross(m, carry):
        r = pl.ds(pl.multiple_of(m * 256, 256), 256)
        wp[r, :] = dot3(brh[r, :], brl[r, :], ch[pl.ds(0, 768), :], cl[pl.ds(0, 768), :])
        return carry

    lax.fori_loop(0, 4, cross, 0)
    parts = []
    for k, peer in enumerate(peers):
        src = wp.at[pl.ds(pl.multiple_of(peer * 64, 64), 64)]
        copy = remote(src, wr.at[row], bs.at[k], br.at[k], peer, col)
        copy.start()
        parts.append(copy)
    total = piece[...] - wp[pl.ds(pl.multiple_of(row * 64, 64), 64), :]
    for k in range(15):
        mine = wr.at[origins[k]]
        remote(mine, mine, bs.at[k], br.at[k], peers[k], col).wait_recv()
        total -= wr[origins[k]]
    wall[row] = total
    ends = []
    for k, peer in enumerate(peers):
        copy = remote(wall.at[row], wall.at[row], cs.at[k], cr.at[k], peer, col)
        copy.start()
        ends.append(copy)
    for k in range(15):
        mine = wall.at[origins[k]]
        remote(mine, mine, cs.at[k], cr.at[k], peers[k], col).wait_recv()
    vh, vl = split(wall[...].reshape(1024, 128))
    ch[...] = vh
    cl[...] = vl

    def last(m, carry):
        r = pl.ds(pl.multiple_of(m * 256, 256), 256)
        diag[r, :] = dot3(th[r, :], tl[r, :], ch[...], cl[...])
        return carry

    lax.fori_loop(0, 4, last, 0)
    for copy in tiles + parts + ends:
        copy.wait_send()


def shape(dims, dtype=F32):
    return jax.ShapeDtypeStruct(dims, dtype)


def shards(ancestor_inv, update_tiles, tile_slot, lower_below, diag_factor):
    lh, ll, th, tl, piece, table = pl.pallas_call(
        prepare,
        out_shape=[shape((JW, JW), BF16)] * 4 + [shape((64, 128)), shape((64,), jnp.int32)],
        in_specs=[SMEM, SMEM, VMEM],
        out_specs=[VMEM] * 5 + [SMEM],
        scratch_shapes=[pltpu.VMEM((JW, JW), F32), pltpu.SMEM((16,), jnp.int32)],
        compiler_params=pltpu.CompilerParams(vmem_limit_bytes=LIMIT),
        name="prepare",
    )(update_tiles, tile_slot, diag_factor)

    def fast(ancestor_inv, update_tiles, tile_slot, lower_below, diag_factor):
        vm = pltpu.VMEM
        dma = pltpu.SemaphoreType.DMA
        cov_o, bro = pl.pallas_call(
            front,
            out_shape=[shape((6, 128, 128)), shape((16, 384, 128))],
            in_specs=[SMEM, ANY, VMEM, VMEM, VMEM],
            out_specs=[VMEM, ANY],
            scratch_shapes=[
                vm((24, 12, 128, 128), F32), vm((16, 768, 128), F32), vm((768, 1536), BF16), vm((768, 1536), BF16),
                vm((768, 256), BF16), vm((768, 256), BF16), vm((4, 768, 256), F32), vm((4, 768, 256), F32),
                vm((768, 1024), BF16), vm((768, 1024), BF16), vm((2, 4, 768, 128), F32), vm((4, 768, 128), F32),
                vm((4, 768, 128), F32), vm((2, 384, 128), F32), vm((2, 768, 128), F32), vm((16, 384, 128), F32),
                dma((24,)), dma((40,)), dma((40,)), dma((16, 2)), dma((16, 2)), dma((16, 2)),
                dma((4,)), dma((4,)), dma((6,)), dma((6,)), dma(()),
            ],
            compiler_params=pltpu.CompilerParams(vmem_limit_bytes=LIMIT, collective_id=0, has_side_effects=True),
            name="front",
        )(table, ancestor_inv.reshape(12, 128, 3072), lower_below, lh, ll)
        return pl.pallas_call(
            back,
            out_shape=[shape((768, 128)), shape((1024, 128))],
            in_specs=[SMEM] + [VMEM] * 5,
            out_specs=[VMEM, VMEM],
            scratch_shapes=[
                vm((16, 128, 128), F32), vm((16, 128, 128), F32), vm((1024, 768), BF16), vm((1024, 768), BF16),
                vm((1024, 128), F32), vm((64, 128), F32), vm((16, 64, 128), F32), vm((16, 64, 128), F32),
                vm((1024, 128), BF16), vm((1024, 128), BF16),
            ] + [dma((15,))] * 6,
            compiler_params=pltpu.CompilerParams(vmem_limit_bytes=LIMIT, collective_id=1, has_side_effects=True),
            name="back",
        )(table, cov_o, bro, th, tl, piece)

    return lax.cond(
        table[OVER] == 0, fast, general, ancestor_inv, update_tiles, tile_slot, lower_below, diag_factor
    )


def solution(mesh):
    in_specs = (P("row", "col"), P(), P(), P("col", "row"), P())
    out_specs = (P("row", "col"), P(None, "col"))
    return jax.shard_map(shards, mesh=mesh, in_specs=in_specs, out_specs=out_specs, check_vma=False)
```

```python
import jax
import jax.numpy as jnp
from jax import lax
from jax.experimental import pallas as pl
from jax.experimental.pallas import tpu as pltpu
from jax.sharding import PartitionSpec as P

TILE = 128
ATILES = 192
UTILES = 96
JW = 1024
MESH = pl.DeviceIdType.MESH
F32, BF16 = jnp.float32, jnp.bfloat16
VMEM = pl.BlockSpec(memory_space=pltpu.VMEM)
SMEM = pl.BlockSpec(memory_space=pltpu.SMEM)
ANY = pl.BlockSpec(memory_space=pl.ANY)
LIMIT = 60 * 1024 * 1024
ROWS, COLS, SLOT, FROM, OVER = 0, 8, 20, 36, 42
FULL, LOW, HIGH = (0, 32), (0, 16), (16, 16)


def spread(value, axis, root):
    mine = lax.axis_index(axis) == root
    return lax.psum(jnp.where(mine, value, jnp.zeros_like(value)), axis)


def solve_right(rows, factor):
    return jax.scipy.linalg.solve_triangular(factor, rows.T, lower=True, trans=1).T


def general(ancestor_inv, update_tiles, tile_slot, lower_below, diag_factor):
    rows_count = lax.axis_size("row")
    cols_count = lax.axis_size("col")
    this_row = lax.axis_index("row")
    this_col = lax.axis_index("col")
    share_rows = UTILES // rows_count
    share_cols = UTILES // cols_count
    slots_dev = ATILES // rows_count
    block_cols = ATILES // cols_count
    capacity = (share_rows + rows_count - 1) // rows_count
    narrow = JW // cols_count
    exact = lax.Precision.HIGHEST
    gathered = lax.all_gather(lower_below, "row", axis=1, tiled=True)
    scaled = solve_right(gathered, diag_factor)
    positions = jnp.arange(UTILES, dtype=jnp.int32)
    slot_of = jnp.take(tile_slot, update_tiles)
    owner_of = slot_of // slots_dev
    target_of = positions // share_rows
    same_group = (
        (owner_of[:, None] == owner_of[None, :])
        & (target_of[:, None] == target_of[None, :])
        & (positions[None, :] < positions[:, None])
    )
    rank_of = jnp.sum(same_group.astype(jnp.int32), axis=1)
    send_slots = jnp.arange(rows_count * capacity, dtype=jnp.int32)
    target_ids = send_slots // capacity
    rank_ids = send_slots % capacity
    matches = (
        (target_of[None, :] == target_ids[:, None])
        & (owner_of[None, :] == this_row)
        & (rank_of[None, :] == rank_ids[:, None])
    )
    local_slot = jnp.sum(jnp.where(matches, slot_of[None, :] - this_row * slots_dev, 0), axis=1)
    present = jnp.any(matches, axis=1).astype(jnp.float32)
    col_tiles = (
        lax.dynamic_slice_in_dim(update_tiles, this_col * share_cols, share_cols)
        - this_col * block_cols
    )
    tiled = ancestor_inv.reshape(slots_dev * TILE, block_cols, TILE)
    local_cols = jnp.take(tiled, col_tiles, axis=1).reshape(slots_dev, TILE, share_cols * TILE)
    own_positions = lax.dynamic_slice_in_dim(positions, this_row * share_rows, share_rows)
    arrival = jnp.take(owner_of, own_positions) * capacity + jnp.take(rank_of, own_positions)
    outgoing = jnp.take(local_cols, local_slot, axis=0) * present[:, None, None]
    incoming = lax.all_to_all(outgoing, "row", split_axis=0, concat_axis=0, tiled=True)
    front_tiles = jnp.take(incoming, arrival, axis=0).reshape(share_rows * TILE, share_cols * TILE)
    row_terms = jnp.dot(front_tiles, scaled, precision=exact)
    cov_below = -lax.psum_scatter(row_terms, "col", scatter_dimension=1, tiled=True)
    root = this_row * share_rows // share_cols
    start = this_row * share_rows % share_cols * TILE
    own_scaled = lax.dynamic_slice_in_dim(scaled, start, share_rows * TILE, 0)
    front_scaled = spread(own_scaled, "col", root)
    columns = (
        jnp.arange(JW, dtype=jnp.int32)[:, None]
        == this_col * narrow + jnp.arange(narrow, dtype=jnp.int32)[None, :]
    ).astype(jnp.float32)
    half_solve = jax.scipy.linalg.solve_triangular(diag_factor, columns, lower=True)
    diag_inverse = jax.scipy.linalg.solve_triangular(diag_factor, half_solve, lower=True, trans=1)
    cross = lax.psum(jnp.dot(front_scaled.T, cov_below, precision=exact), "row")
    cov_diag = diag_inverse - cross
    return (cov_below, cov_diag)


def split(value):
    high = value.astype(BF16)
    return high, (value - high.astype(F32)).astype(BF16)


def dot3(ah, al, bh, bl):
    out = jnp.dot(ah, bh, preferred_element_type=F32)
    out += jnp.dot(ah, bl, preferred_element_type=F32)
    return out + jnp.dot(al, bh, preferred_element_type=F32)


def remote(src, dst, send, recv, row, col):
    return pltpu.make_async_remote_copy(
        src_ref=src, dst_ref=dst, send_sem=send, recv_sem=recv, device_id=(row, col), device_id_type=MESH
    )


def greet(peers):
    barrier = pltpu.get_barrier_semaphore()
    for peer in peers:
        pl.semaphore_signal(barrier, inc=1, device_id=peer, device_id_type=MESH)
    pl.semaphore_wait(barrier, len(peers))


def tables(upd, slots, table, counts):
    row, col = lax.axis_index("row"), lax.axis_index("col")
    for i in range(64):
        table[i] = 0
    for i in range(16):
        counts[i] = 0

    def visit(u, carry):
        slot = slots[upd[u]]
        owner = slot // 12
        seen = counts[owner]
        counts[owner] = seen + 1

        @pl.when(seen >= 6)
        def _():
            table[OVER] = 1

        @pl.when((owner == row) & (seen < 6))
        def _():
            table[ROWS + seen] = slot - 12 * row
            table[SLOT + u // 6] = seen

        return carry

    lax.fori_loop(0, UTILES, visit, 0)
    for k in range(12):
        table[COLS + k] = upd[12 * col + k] - 24 * col
    for i in range(6):
        table[FROM + i] = slots[upd[6 * row + i]] // 12


ITEMS = (
    (0, 0), (0, -1), (0, 1), (-1, 0), (1, 0), (0, 2), (2, 0), (-1, -1),
    (1, -1), (-1, 1), (1, 1), (-1, 2), (1, 2), (2, -1), (2, 1), (2, 2),
)


def work(
    table, anc, lbt, diag, cov, cov_diag,
    ancv, bg, sh, sl, bh, bl, ph, pq, qr, d2r, d1r, brx, dg, inv, lh, ll,
    co, slots, inc, wp, wr, wall, ch, cl,
    anc_sem, own_sem, dg_sem, gs, gr, xs, ps, sr, es, er, rs, rr, is_, ir, as_, ar, bs, br, cs, cr,
):
    row, col = lax.axis_index("row"), lax.axis_index("col")
    y, z, x, core = row // 4, row % 4, col // 2, col % 2
    other = 2 * x + 1 - core

    def at(dy, dz):
        return 4 * lax.rem(y + dy + 4, 4) + lax.rem(z + dz + 4, 4)

    def along(dx):
        return 2 * lax.rem(x + dx + 4, 4) + core

    own = pltpu.make_async_copy(lbt, bg.at[row], own_sem)
    own.start()
    dg_load = pltpu.make_async_copy(diag, dg, dg_sem)
    dg_load.start()
    loads = [
        pltpu.make_async_copy(anc.at[:, :, pl.ds(128 * t, 128)], ancv.at[t], anc_sem.at[t])
        for t in range(24)
    ]
    for load in loads:
        load.start()
    peers = [lax.rem(row + d, 16) for d in range(1, 16)]
    origins = [lax.rem(row + 16 - d, 16) for d in range(1, 16)]
    greet([(peer, col) for peer in peers] + [(row, along(1)), (row, along(-1)), (row, other)])
    own.wait()

    def rel(h, a, b):
        return at(a, b) if h == 0 else at(b, a)

    ids = {}
    sends = []

    def gather(name, h, src, rows, step, recv_src):
        k = ids.setdefault((h, name), len(ids))
        part = pl.ds(32 * h + rows[0], rows[1])
        view = bg.at[rel(h, *src), part]
        copy = remote(view, view, gs.at[k], gr.at[k], rel(h, *step), col)
        copy.start()
        mine = bg.at[rel(h, *recv_src), part]
        got = remote(mine, mine, gs.at[k], gr.at[k], rel(h, *step), col)
        sends.append(copy)
        return got

    arr = {}

    def first_phase(h):
        arr[h, 0, -1] = [gather("f+", h, (0, 0), FULL, (0, 1), (0, -1))]
        arr[h, 0, 1] = [gather("f-", h, (0, 0), FULL, (0, -1), (0, 1))]

    def first_forward(h):
        arr[h, 0, 2] = [
            gather("ff+", h, (0, -1), LOW, (0, 1), (0, -2)),
            gather("ff-", h, (0, 1), HIGH, (0, -1), (0, 2)),
        ]

    def second_phase(h, q):
        arr[h, -1, q] = [gather(("s+", q), h, (0, q), FULL, (1, 0), (-1, q))]
        arr[h, 1, q] = [gather(("s-", q), h, (0, q), FULL, (-1, 0), (1, q))]

    def second_forward(h, q):
        arr[h, 2, q] = [
            gather(("sf+", q), h, (-1, q), LOW, (1, 0), (-2, q)),
            gather(("sf-", q), h, (1, q), HIGH, (-1, 0), (2, q)),
        ]

    def wait(h, a, b):
        for got in arr[h, a, b]:
            got.wait_recv()

    parity = row % 2
    root_x, root_core = row // 4, (row // 2) % 2
    dist = lax.rem(x - root_x + 4, 4)
    ring = core == root_core

    def spread_copies(i):
        def make(h, device):
            view = brx.at[i, pl.ds(32 * h, 32)]
            return remote(view, view, xs.at[i, h], sr.at[i, h], row, device)

        def partner(h):
            view = brx.at[i, pl.ds(32 * h, 32)]
            return remote(view, view, ps.at[i, h], sr.at[i, h], row, other)

        return make(0, along(1)), make(1, along(-1)), partner(0), partner(1)

    def spread_root(i):
        @pl.when(ring & (dist == 0))
        def _():
            lanes = pl.ds(pl.multiple_of(768 * parity, 768), 768)
            for h in range(2):
                brx[i, pl.ds(32 * h, 32), :] = bg[rel(h, *ITEMS[i]), pl.ds(32 * h, 32), lanes]
            for copy in spread_copies(i):
                copy.start()

    def spread_hop(i, hop):
        up, down, pup, pdown = spread_copies(i)

        @pl.when(ring & (dist == hop))
        def _():
            up.wait_recv()
            if hop < 3:
                up.start()
            pup.start()

        @pl.when(ring & (dist == 4 - hop))
        def _():
            down.wait_recv()
            if hop < 3:
                down.start()
            pdown.start()

    def spread_end(i):
        up, down, pup, pdown = spread_copies(i)

        @pl.when(ring)
        def _():
            pup.wait_send()
            pdown.wait_send()

            @pl.when(dist != 3)
            def _():
                up.wait_send()

            @pl.when(dist != 1)
            def _():
                down.wait_send()

        @pl.when(jnp.logical_not(ring))
        def _():
            pup.wait_recv()
            pdown.wait_recv()

    def spread_step(i):
        if i < 16:
            spread_root(i)
        for hop in (1, 2, 3):
            if 0 <= i - hop < 16:
                spread_hop(i - hop, hop)

    def extract(j, carry):
        for k in range(12):
            high, low = split(ancv[table[COLS + k], table[ROWS + j]])
            c = pl.ds(128 * k, 128)
            for half in range(2):
                dst = pl.ds(pl.multiple_of(384 * half + j * 64, 64), 64)
                sh[dst, c] = high[64 * half : 64 * half + 64]
                sl[dst, c] = low[64 * half : 64 * half + 64]
        return carry

    base = pl.multiple_of(512 * core, 512)
    i256 = lax.broadcasted_iota(jnp.int32, (256, 256), 0)
    j256 = lax.broadcasted_iota(jnp.int32, (256, 256), 1)

    def sub(b, size):
        return pl.ds(pl.multiple_of(base + size * b, size), size)

    def inverse_start():
        dg_load.wait()
        inv[pl.ds(0, 512), pl.ds(512, 512)] = jnp.zeros((512, 512), F32)
        inv[sub(0, 256), sub(1, 256)] = jnp.zeros((256, 256), F32)
        for b in range(2):
            s = sub(b, 256)
            inv[s, s] = jnp.where(i256 == j256, 1.0 / dg[s, s], 0.0)

    def inverse_levels(first, last):
        def level(n, carry):
            bi, bj = lax.shift_right_logical(i256, n), lax.shift_right_logical(j256, n)
            mask = (bi == bj + 1) & ((bi & 1) == 1)
            for b in range(2):
                s = sub(b, 256)
                value = inv[s, s]
                part = split(value)
                inner = dot3(*split(jnp.where(mask, dg[s, s], 0.0)), *part)
                inv[s, s] = value - dot3(*part, *split(inner))
            return carry

        lax.fori_loop(first, last, level, 0)

    swap_inv = []

    def inverse_512():
        top, low = sub(0, 256), sub(1, 256)
        inner = dot3(*split(dg[low, top]), *split(inv[top, top]))
        inv[low, top] = -dot3(*split(inv[low, low]), *split(inner))
        block = inv.at[pl.ds(base, 512), pl.ds(base, 512)]
        copy = remote(block, block, is_, ir, row, other)
        copy.start()
        swap_inv.append(copy)

    def inverse_1024():
        there = pl.ds(pl.multiple_of(512 - base, 512), 512)
        block = inv.at[there, there]
        remote(block, block, is_, ir, row, other).wait_recv()
        top, low = pl.ds(0, 512), pl.ds(512, 512)
        xh, xl = split(inv[top, top])
        for m in range(2):
            r = pl.ds(512 + 256 * m, 256)
            inner = dot3(*split(dg[r, top]), xh, xl)
            dg[r, top] = inner
        ih, il = split(dg[low, top])
        for m in range(2):
            r = pl.ds(512 + 256 * m, 256)
            inv[r, top] = -dot3(*split(inv[r, low]), ih, il)

    def inverse_rows():
        for i, item in enumerate(ITEMS):
            for h in range(2):
                src = pl.ds(pl.multiple_of(64 * rel(h, *item) + 32 * h, 32), 32)
                dst = pl.ds(64 * i + 32 * h, 32)
                lh[dst, :], ll[dst, :] = split(inv[src, :])

    def build(g):
        for p in range(2):
            for k in range(12):
                lanes = pl.ds(128 * k, 128)
                rows = [
                    bg[rel(h, *ITEMS[4 * g + 2 * p + i]), pl.ds(32 * h, 32), lanes]
                    for i in range(2)
                    for h in range(2)
                ]
                c = pl.ds(128 * p, 128)
                bh[lanes, c], bl[lanes, c] = split(jnp.concatenate(rows, axis=0).T)

    def product(g, chunk):
        r = pl.ds(384 * chunk, 384)
        c = pl.ds(256 * g, 256)
        ph[r, c], pq[r, c] = split(dot3(sh[r, :], sl[r, :], bh[...], bl[...]))

    def group(g):
        build(g)
        for chunk in range(2):
            product(g, chunk)

    def block(dx):
        return pl.ds(pl.multiple_of(256 * lax.rem(x + dx + 4, 4), 256), 256)

    DX = (2, 1, -1, 0)
    EARLY, LATE = pl.ds(0, 768), pl.ds(768, 256)

    def early_columns(k):
        c = block(DX[k])
        for chunk in range(2):
            r = pl.ds(384 * chunk, 384)
            acc = dot3(ph[r, EARLY], pq[r, EARLY], lh[EARLY, c], ll[EARLY, c])
            for half in range(2):
                ancv[2 * k + half, pl.ds(3 * chunk, 3)] = acc[:, 128 * half : 128 * half + 128].reshape(3, 128, 128)

    both = (0, 1)
    for h in both:
        first_phase(h)
    for h in both:
        second_phase(h, 0)
    spread_step(0)
    inverse_start()
    inverse_levels(0, 4)
    for q in (-1, 1):
        for h in both:
            wait(h, 0, q)
        if q == 1:
            for h in both:
                first_forward(h)
        for h in both:
            second_phase(h, q)
    spread_step(1)
    spread_step(2)
    for load in loads:
        load.wait()
    lax.fori_loop(0, 6, extract, 0)
    for h in both:
        wait(h, -1, 0)
        wait(h, 1, 0)
        second_forward(h, 0)
    spread_step(3)
    spread_step(4)
    inverse_levels(4, 8)
    for h in both:
        wait(h, 0, 2)
        second_phase(h, 2)
    spread_step(5)
    inverse_512()
    for h in both:
        wait(h, 2, 0)
    spread_step(6)
    for q, i in ((-1, 7), (1, 9)):
        for h in both:
            wait(h, -1, q)
            wait(h, 1, q)
            second_forward(h, q)
        spread_step(i)
        spread_step(i + 1)
        group(0 if q == -1 else 1)
    inverse_1024()
    inverse_rows()
    for h in both:
        wait(h, -1, 2)
        wait(h, 1, 2)
        second_forward(h, 2)
    spread_step(11)
    spread_step(12)
    group(2)
    for h in both:
        wait(h, 2, -1)
        wait(h, 2, 1)
    spread_step(13)
    spread_step(14)
    for k in range(4):
        early_columns(k)
    for h in both:
        wait(h, 2, 2)
    spread_step(15)
    build(3)

    UPPER, LOWER = pl.ds(0, 64), pl.ds(64, 64)
    swaps, moves = {}, {}

    def tiles(chunk):
        return pl.ds(3 * chunk, 3)

    def columns(chunk, k):
        r = pl.ds(384 * chunk, 384)
        c = block(DX[k])
        acc = dot3(ph[r, LATE], pq[r, LATE], lh[LATE, c], ll[LATE, c])
        for half in range(2):
            part = acc[:, 128 * half : 128 * half + 128].reshape(3, 128, 128)
            ancv[8 + 4 * half + k, tiles(chunk)] = ancv[2 * k + half, tiles(chunk)] + part
        copy = remote(
            ancv.at[8 + 4 * (1 - core) + k, tiles(chunk)], qr.at[k, tiles(chunk)],
            es.at[chunk, k], er.at[chunk, k], row, other,
        )
        copy.start()
        swaps[chunk, k] = copy

    def merged(chunk, k):
        swaps[chunk, k].wait_recv()
        ancv[16 + k, tiles(chunk)] = ancv[8 + 4 * core + k, tiles(chunk)] + qr[k, tiles(chunk)]

    def move(chunk, n, k, part, dst, dx):
        copy = remote(
            ancv.at[16 + k, tiles(chunk), part], dst, rs.at[chunk, n], rr.at[chunk, n], row, along(dx)
        )
        copy.start()
        moves[chunk, n] = copy

    def far(chunk):
        move(chunk, 0, 0, UPPER, d2r.at[chunk, 0], 1)
        move(chunk, 1, 0, LOWER, d2r.at[chunk, 1], -1)

    def near_up(chunk):
        move(chunk, 2, 1, LOWER, d1r.at[chunk, 0, :, LOWER], 1)

    def near_down(chunk):
        move(chunk, 3, 2, UPPER, d1r.at[chunk, 1, :, UPPER], -1)

    def passed(chunk):
        moves[chunk, 0].wait_recv()
        ancv[17, tiles(chunk), UPPER] += d2r[chunk, 0]
        move(chunk, 4, 1, UPPER, d1r.at[chunk, 0, :, UPPER], 1)
        moves[chunk, 1].wait_recv()
        ancv[18, tiles(chunk), LOWER] += d2r[chunk, 1]
        move(chunk, 5, 2, LOWER, d1r.at[chunk, 1, :, LOWER], -1)

    tile_copies = {}

    def finish(chunk):
        for n in (2, 3, 4, 5):
            moves[chunk, n].wait_recv()
        for t in range(3):
            total = -(ancv[19, 3 * chunk + t] + d1r[chunk, 0, t] + d1r[chunk, 1, t])
            co[chunk, 2 * t] = total[:64]
            co[chunk, 2 * t + 1] = total[64:]
        for t in range(16):
            slots[chunk, t] = co[chunk, table[SLOT + t]]
        for k, peer in enumerate(peers):
            copy = remote(slots.at[chunk, peer], inc.at[chunk, row], as_.at[chunk, k], ar.at[chunk, k], peer, col)
            copy.start()
            tile_copies[chunk, k] = copy
        inc[chunk, row] = slots[chunk, row]

    product(3, 0)
    columns(0, 0)
    columns(0, 1)
    merged(0, 0)
    far(0)
    columns(0, 2)
    merged(0, 1)
    near_up(0)
    columns(0, 3)
    merged(0, 2)
    near_down(0)
    spread_step(16)
    product(3, 1)
    merged(0, 3)
    columns(1, 0)
    passed(0)
    columns(1, 1)
    merged(1, 0)
    far(1)
    columns(1, 2)
    merged(1, 1)
    near_up(1)
    columns(1, 3)
    merged(1, 2)
    near_down(1)
    merged(1, 3)
    spread_step(17)
    finish(0)
    passed(1)
    spread_step(18)
    for i in range(16):
        spread_end(i)
    for m in range(8):
        s = pl.ds(128 * m, 128)
        lh[:, s], ll[:, s] = split(inv[s, :].T)
    finish(1)

    for chunk in range(2):
        for k in range(15):
            mine = inc.at[chunk, origins[k]]
            remote(mine, mine, as_.at[chunk, k], ar.at[chunk, k], peers[k], col).wait_recv()
    for i in range(6):
        for half in range(2):
            tile = inc[half, table[FROM + i]]
            r = pl.ds(128 * i + 64 * half, 64)
            cov[r, :] = tile
            ch[r, :], cl[r, :] = split(tile)
    for m in range(4):
        rows = brx[pl.ds(4 * m, 4)].reshape(256, 768)
        part = dot3(*split(rows), ch[pl.ds(0, 768), :], cl[pl.ds(0, 768), :])
        for i in range(4):
            for h in range(2):
                dst = pl.ds(pl.multiple_of(64 * rel(h, *ITEMS[4 * m + i]) + 32 * h, 32), 32)
                wp[dst, :] = part[64 * i + 32 * h : 64 * i + 32 * h + 32]
    parts = []
    for k, peer in enumerate(peers):
        src = wp.at[pl.ds(pl.multiple_of(peer * 64, 64), 64)]
        copy = remote(src, wr.at[row], bs.at[k], br.at[k], peer, col)
        copy.start()
        parts.append(copy)
    here = pl.ds(pl.multiple_of(row * 64, 64), 64)
    total = inv[here, pl.ds(pl.multiple_of(col * 128, 128), 128)] - wp[here, :]
    for k in range(15):
        mine = wr.at[origins[k]]
        remote(mine, mine, bs.at[k], br.at[k], peers[k], col).wait_recv()
        total -= wr[origins[k]]
    wall[row] = total
    ends = []
    for k, peer in enumerate(peers):
        copy = remote(wall.at[row], wall.at[row], cs.at[k], cr.at[k], peer, col)
        copy.start()
        ends.append(copy)
    for k in range(15):
        mine = wall.at[origins[k]]
        remote(mine, mine, cs.at[k], cr.at[k], peers[k], col).wait_recv()
    ch[...], cl[...] = split(wall[...].reshape(1024, 128))
    for m in range(4):
        r = pl.ds(256 * m, 256)
        cov_diag[r, :] = dot3(lh[r, :], ll[r, :], ch[...], cl[...])
    for copy in sends + swap_inv + list(swaps.values()) + list(moves.values()) + list(tile_copies.values()):
        copy.wait_send()
    for copy in parts + ends:
        copy.wait_send()


def shape(dims, dtype=F32):
    return jax.ShapeDtypeStruct(dims, dtype)


def shards(ancestor_inv, update_tiles, tile_slot, lower_below, diag_factor):
    table = pl.pallas_call(
        tables,
        out_shape=shape((64,), jnp.int32),
        in_specs=[SMEM, SMEM],
        out_specs=SMEM,
        scratch_shapes=[pltpu.SMEM((16,), jnp.int32)],
        name="tables",
    )(update_tiles, tile_slot)

    def fast(ancestor_inv, update_tiles, tile_slot, lower_below, diag_factor):
        vm = pltpu.VMEM
        dma = pltpu.SemaphoreType.DMA
        return pl.pallas_call(
            work,
            out_shape=[shape((768, 128)), shape((1024, 128))],
            in_specs=[SMEM, ANY, ANY, ANY],
            out_specs=[VMEM, VMEM],
            scratch_shapes=[
                vm((24, 12, 128, 128), F32), vm((16, 64, 1536), F32), vm((768, 1536), BF16), vm((768, 1536), BF16),
                vm((1536, 256), BF16), vm((1536, 256), BF16), vm((768, 1024), BF16), vm((768, 1024), BF16),
                vm((4, 6, 128, 128), F32), vm((2, 2, 3, 64, 128), F32), vm((2, 2, 3, 128, 128), F32),
                vm((16, 64, 768), F32), vm((1024, 1024), F32), vm((1024, 1024), F32), vm((1024, 1024), BF16),
                vm((1024, 1024), BF16), vm((2, 6, 64, 128), F32), vm((2, 16, 64, 128), F32), vm((2, 16, 64, 128), F32),
                vm((1024, 128), F32), vm((16, 64, 128), F32), vm((16, 64, 128), F32), vm((1024, 128), BF16),
                vm((1024, 128), BF16),
                dma((24,)), dma(()), dma(()), dma((40,)), dma((40,)), dma((16, 2)), dma((16, 2)), dma((16, 2)),
                dma((2, 4)), dma((2, 4)), dma((2, 6)), dma((2, 6)), dma(()), dma(()), dma((2, 15)), dma((2, 15)),
                dma((15,)), dma((15,)), dma((15,)), dma((15,)),
            ],
            compiler_params=pltpu.CompilerParams(vmem_limit_bytes=LIMIT, collective_id=0, has_side_effects=True),
            name="work",
        )(table, ancestor_inv.reshape(12, 128, 3072), lower_below.T, diag_factor)

    return lax.cond(
        table[OVER] == 0, fast, general, ancestor_inv, update_tiles, tile_slot, lower_below, diag_factor
    )


def solution(mesh):
    in_specs = (P("row", "col"), P(), P(), P("col", "row"), P())
    out_specs = (P("row", "col"), P(None, "col"))
    return jax.shard_map(shards, mesh=mesh, in_specs=in_specs, out_specs=out_specs, check_vma=False)
```

```python
import jax
import jax.numpy as jnp
from jax import lax
from jax.experimental import pallas as pl
from jax.experimental.pallas import tpu as pltpu
from jax.sharding import PartitionSpec as P

TILE = 128
ATILES = 192
UTILES = 96
JW = 1024
MESH = pl.DeviceIdType.MESH
F32, BF16 = jnp.float32, jnp.bfloat16
VMEM = pl.BlockSpec(memory_space=pltpu.VMEM)
SMEM = pl.BlockSpec(memory_space=pltpu.SMEM)
ANY = pl.BlockSpec(memory_space=pl.ANY)
LIMIT = 60 * 1024 * 1024
ROWS, COLS, SLOT, FROM, KEEP, TURN = 0, 8, 20, 36, 42, 48
FULL, LOW, HIGH = (0, 32), (0, 16), (16, 16)


def split(value):
    high = value.astype(BF16)
    return high, (value - high.astype(F32)).astype(BF16)


def dot3(ah, al, bh, bl):
    out = jnp.dot(ah, bh, preferred_element_type=F32)
    out += jnp.dot(ah, bl, preferred_element_type=F32)
    return out + jnp.dot(al, bh, preferred_element_type=F32)


def remote(src, dst, send, recv, row, col):
    return pltpu.make_async_remote_copy(
        src_ref=src, dst_ref=dst, send_sem=send, recv_sem=recv, device_id=(row, col), device_id_type=MESH
    )


def greet(peers, more, far, extra):
    barrier = pltpu.get_barrier_semaphore()
    for peer in peers:
        pl.semaphore_signal(barrier, inc=1, device_id=peer, device_id_type=MESH)

    @pl.when(more)
    def _():
        pl.semaphore_signal(barrier, inc=1, device_id=far, device_id_type=MESH)

    pl.semaphore_wait(barrier, len(peers) + extra)


def tables(upd, slots, first, second, more, counts):
    row, col = lax.axis_index("row"), lax.axis_index("col")
    more[0] = 0
    for i in range(16):
        counts[i] = 0
    for turn, table in enumerate((first, second)):
        for i in range(48):
            table[i] = 0
        for k in range(12):
            table[COLS + k] = upd[12 * col + k] - 24 * col
        table[TURN] = turn

    def visit(u, carry):
        slot = slots[upd[u]]
        owner = slot // 12
        seen = counts[owner]
        counts[owner] = seen + 1
        target = u // 6

        @pl.when(seen >= 6)
        def _():
            more[0] = 1

        @pl.when(owner == row)
        def _():
            for turn, table in enumerate((first, second)):

                @pl.when(seen // 6 == turn)
                def _():
                    table[ROWS + seen - 6 * turn] = slot - 12 * row
                    table[SLOT + target] = seen - 6 * turn

        @pl.when(target == row)
        def _():
            for turn, table in enumerate((first, second)):
                table[FROM + u - 6 * row] = owner
                table[KEEP + u - 6 * row] = jnp.where(seen // 6 == turn, 1, 0)

        return carry

    lax.fori_loop(0, UTILES, visit, 0)


ITEMS = (
    (0, 0), (0, -1), (0, 1), (-1, 0), (1, 0), (0, 2), (2, 0), (-1, -1),
    (1, -1), (-1, 1), (1, 1), (-1, 2), (1, 2), (2, -1), (2, 1), (2, 2),
)


def work(
    table, anc, lbt, diag, cov, cov_diag,
    ancv, bg, sh, sl, bh, bl, ph, pq, qr, d2r, d1r, brx, dg, inv, lh, ll,
    co, slots, inc, wp, w1, s1, w2, g1, wall, ch, cl,
    anc_sem, own_sem, dg_sem, gs, gr, xs, sr, ss, sg, ps, pr, es, er, rs, rr, is_, ir, as_, ar, bs, br,
):
    row, col = lax.axis_index("row"), lax.axis_index("col")
    y, z, x, core = row // 4, row % 4, col // 2, col % 2
    other = 2 * x + 1 - core

    def at(dy, dz):
        return 4 * lax.rem(y + dy + 4, 4) + lax.rem(z + dz + 4, 4)

    def along(dx):
        return 2 * lax.rem(x + dx + 4, 4) + core

    own = pltpu.make_async_copy(lbt, bg.at[row], own_sem)
    own.start()
    dg_load = pltpu.make_async_copy(diag, dg, dg_sem)
    dg_load.start()
    loads = [
        pltpu.make_async_copy(anc.at[:, :, pl.ds(128 * t, 128)], ancv.at[t], anc_sem.at[t])
        for t in range(24)
    ]
    for load in loads:
        load.start()
    peers = [lax.rem(row + d, 16) for d in range(1, 16)]
    origins = [lax.rem(row + 16 - d, 16) for d in range(1, 16)]
    parity = row % 2
    root_x, root_core = row // 4, (row // 2) % 2
    dist = lax.rem(x - root_x + 4, 4)
    ring = core == root_core
    opposite = jnp.where(ring & (dist != 2), 1, 0)
    greet(
        [(peer, col) for peer in peers] + [(row, along(1)), (row, along(-1)), (row, other)],
        ring & (dist != 0), (row, along(2)), opposite,
    )
    own.wait()

    def rel(h, a, b):
        return at(a, b) if h == 0 else at(b, a)

    ids = {}
    sends = []

    def gather(name, h, src, rows, step, recv_src):
        k = ids.setdefault((h, name), len(ids))
        part = pl.ds(32 * h + rows[0], rows[1])
        view = bg.at[rel(h, *src), part]
        copy = remote(view, view, gs.at[k], gr.at[k], rel(h, *step), col)
        copy.start()
        mine = bg.at[rel(h, *recv_src), part]
        got = remote(mine, mine, gs.at[k], gr.at[k], rel(h, *step), col)
        sends.append(copy)
        return got

    arr = {}

    def first_phase(h):
        arr[h, 0, -1] = [gather("f+", h, (0, 0), FULL, (0, 1), (0, -1))]
        arr[h, 0, 1] = [gather("f-", h, (0, 0), FULL, (0, -1), (0, 1))]

    def first_forward(h):
        arr[h, 0, 2] = [
            gather("ff+", h, (0, -1), LOW, (0, 1), (0, -2)),
            gather("ff-", h, (0, 1), HIGH, (0, -1), (0, 2)),
        ]

    def second_phase(h, q):
        arr[h, -1, q] = [gather(("s+", q), h, (0, q), FULL, (1, 0), (-1, q))]
        arr[h, 1, q] = [gather(("s-", q), h, (0, q), FULL, (-1, 0), (1, q))]

    def second_forward(h, q):
        arr[h, 2, q] = [
            gather(("sf+", q), h, (-1, q), LOW, (1, 0), (-2, q)),
            gather(("sf-", q), h, (1, q), HIGH, (-1, 0), (2, q)),
        ]

    def wait(h, a, b):
        for got in arr[h, a, b]:
            got.wait_recv()

    def quarter(d):
        return pl.ds(pl.multiple_of(16 * d, 16), 16)

    def chip(d):
        return 2 * lax.rem(root_x + d, 4) + root_core

    def scatter_copy(i, d):
        view = brx.at[i, quarter(d)]
        return remote(view, view, xs.at[i, d - 1], sr.at[i], row, chip(d))

    def scatter(i):
        @pl.when(ring & (dist == 0))
        def _():
            lanes = pl.ds(pl.multiple_of(768 * parity, 768), 768)
            for h in range(2):
                brx[i, pl.ds(32 * h, 32), :] = bg[rel(h, *ITEMS[i]), pl.ds(32 * h, 32), lanes]
            for d in (1, 2, 3):
                scatter_copy(i, d).start()

    def batch(b):
        return pl.ds(8 * b, 8)

    def share_copy(b, e):
        view = brx.at[batch(b), quarter(dist)]
        return remote(view, view, ss.at[b, e - 1], sg.at[b, e - 1], row, along(e))

    def share(b):
        for i in range(8 * b, 8 * b + 8):

            @pl.when(ring & (dist != 0))
            def _():
                view = brx.at[i, quarter(dist)]
                remote(view, view, xs.at[i, 0], sr.at[i], row, along(1)).wait_recv()

        for e in (1, 3, 2):

            @pl.when(ring & (lax.rem(dist + e, 4) != 0))
            def _():
                share_copy(b, e).start()

    def partner_copy(b):
        view = brx.at[batch(b)]
        return remote(view, view, ps.at[b], pr.at[b], row, other)

    def hand_over(b):
        @pl.when(ring & (dist != 0))
        def _():
            for e in (1, 2, 3):
                view = brx.at[batch(b), quarter(lax.rem(dist - e + 4, 4))]
                remote(view, view, ss.at[b, e - 1], sg.at[b, e - 1], row, along(e)).wait_recv()

        @pl.when(ring)
        def _():
            partner_copy(b).start()

    def spread_end(b):
        @pl.when(jnp.logical_not(ring))
        def _():
            partner_copy(b).wait_recv()

    def spread_sent():
        for b in range(2):

            @pl.when(ring)
            def _():
                partner_copy(b).wait_send()

            for e in (1, 2, 3):

                @pl.when(ring & (lax.rem(dist + e, 4) != 0))
                def _():
                    share_copy(b, e).wait_send()

        @pl.when(ring & (dist == 0))
        def _():
            for i in range(16):
                for d in (1, 2, 3):
                    scatter_copy(i, d).wait_send()

    def spread_step(i):
        scatter(i)

    def extract(j, carry):
        for k in range(12):
            high, low = split(ancv[table[COLS + k], table[ROWS + j]])
            c = pl.ds(128 * k, 128)
            for half in range(2):
                dst = pl.ds(pl.multiple_of(384 * half + j * 64, 64), 64)
                sh[dst, c] = high[64 * half : 64 * half + 64]
                sl[dst, c] = low[64 * half : 64 * half + 64]
        return carry

    base = pl.multiple_of(512 * core, 512)
    i256 = lax.broadcasted_iota(jnp.int32, (256, 256), 0)
    j256 = lax.broadcasted_iota(jnp.int32, (256, 256), 1)

    def sub(b, size):
        return pl.ds(pl.multiple_of(base + size * b, size), size)

    def inverse_start():
        dg_load.wait()
        inv[pl.ds(0, 512), pl.ds(512, 512)] = jnp.zeros((512, 512), F32)
        inv[sub(0, 256), sub(1, 256)] = jnp.zeros((256, 256), F32)
        for b in range(2):
            s = sub(b, 256)
            inv[s, s] = jnp.where(i256 == j256, 1.0 / dg[s, s], 0.0)

    def inverse_levels(first, last):
        def level(n, carry):
            bi, bj = lax.shift_right_logical(i256, n), lax.shift_right_logical(j256, n)
            mask = (bi == bj + 1) & ((bi & 1) == 1)
            for b in range(2):
                s = sub(b, 256)
                value = inv[s, s]
                part = split(value)
                inner = dot3(*split(jnp.where(mask, dg[s, s], 0.0)), *part)
                inv[s, s] = value - dot3(*part, *split(inner))
            return carry

        lax.fori_loop(first, last, level, 0)

    swap_inv = []

    def inverse_512():
        top, low = sub(0, 256), sub(1, 256)
        inner = dot3(*split(dg[low, top]), *split(inv[top, top]))
        inv[low, top] = -dot3(*split(inv[low, low]), *split(inner))
        block = inv.at[pl.ds(base, 512), pl.ds(base, 512)]
        copy = remote(block, block, is_, ir, row, other)
        copy.start()
        swap_inv.append(copy)

    def inverse_1024():
        there = pl.ds(pl.multiple_of(512 - base, 512), 512)
        block = inv.at[there, there]
        remote(block, block, is_, ir, row, other).wait_recv()
        top, low = pl.ds(0, 512), pl.ds(512, 512)
        xh, xl = split(inv[top, top])
        for m in range(2):
            r = pl.ds(512 + 256 * m, 256)
            inner = dot3(*split(dg[r, top]), xh, xl)
            dg[r, top] = inner
        ih, il = split(dg[low, top])
        for m in range(2):
            r = pl.ds(512 + 256 * m, 256)
            inv[r, top] = -dot3(*split(inv[r, low]), ih, il)

    def inverse_rows():
        for i, item in enumerate(ITEMS):
            for h in range(2):
                src = pl.ds(pl.multiple_of(64 * rel(h, *item) + 32 * h, 32), 32)
                dst = pl.ds(64 * i + 32 * h, 32)
                lh[dst, :], ll[dst, :] = split(inv[src, :])

    def build(g):
        for p in range(2):
            for k in range(12):
                lanes = pl.ds(128 * k, 128)
                rows = [
                    bg[rel(h, *ITEMS[4 * g + 2 * p + i]), pl.ds(32 * h, 32), lanes]
                    for i in range(2)
                    for h in range(2)
                ]
                c = pl.ds(128 * p, 128)
                bh[lanes, c], bl[lanes, c] = split(jnp.concatenate(rows, axis=0).T)

    def product(g, chunk):
        r = pl.ds(384 * chunk, 384)
        c = pl.ds(256 * g, 256)
        ph[r, c], pq[r, c] = split(dot3(sh[r, :], sl[r, :], bh[...], bl[...]))

    def group(g):
        build(g)
        for chunk in range(2):
            product(g, chunk)

    def block(dx):
        return pl.ds(pl.multiple_of(256 * lax.rem(x + dx + 4, 4), 256), 256)

    DX = (2, 1, -1, 0)
    EARLY, LATE = pl.ds(0, 768), pl.ds(768, 256)

    def early_columns(k):
        c = block(DX[k])
        for chunk in range(2):
            r = pl.ds(384 * chunk, 384)
            acc = dot3(ph[r, EARLY], pq[r, EARLY], lh[EARLY, c], ll[EARLY, c])
            for half in range(2):
                ancv[2 * k + half, pl.ds(3 * chunk, 3)] = acc[:, 128 * half : 128 * half + 128].reshape(3, 128, 128)

    both = (0, 1)
    for h in both:
        first_phase(h)
    for h in both:
        second_phase(h, 0)
    spread_step(0)
    inverse_start()
    inverse_levels(0, 4)
    for q in (-1, 1):
        for h in both:
            wait(h, 0, q)
        if q == 1:
            for h in both:
                first_forward(h)
        for h in both:
            second_phase(h, q)
    spread_step(1)
    spread_step(2)
    for load in loads:
        load.wait()
    lax.fori_loop(0, 6, extract, 0)
    for h in both:
        wait(h, -1, 0)
        wait(h, 1, 0)
        second_forward(h, 0)
    spread_step(3)
    spread_step(4)
    inverse_levels(4, 8)
    for h in both:
        wait(h, 0, 2)
        second_phase(h, 2)
    spread_step(5)
    inverse_512()
    for h in both:
        wait(h, 2, 0)
    spread_step(6)
    for q, i in ((-1, 7), (1, 9)):
        for h in both:
            wait(h, -1, q)
            wait(h, 1, q)
            second_forward(h, q)
        spread_step(i)
        spread_step(i + 1)
        group(0 if q == -1 else 1)
    inverse_1024()
    inverse_rows()
    for h in both:
        wait(h, -1, 2)
        wait(h, 1, 2)
        second_forward(h, 2)
    spread_step(11)
    spread_step(12)
    group(2)
    share(0)
    for h in both:
        wait(h, 2, -1)
        wait(h, 2, 1)
    spread_step(13)
    spread_step(14)
    for k in range(4):
        early_columns(k)
    for h in both:
        wait(h, 2, 2)
    spread_step(15)
    build(3)

    UPPER, LOWER = pl.ds(0, 64), pl.ds(64, 64)
    swaps, moves = {}, {}

    def tiles(chunk):
        return pl.ds(3 * chunk, 3)

    def columns(chunk, k):
        r = pl.ds(384 * chunk, 384)
        c = block(DX[k])
        acc = dot3(ph[r, LATE], pq[r, LATE], lh[LATE, c], ll[LATE, c])
        for half in range(2):
            part = acc[:, 128 * half : 128 * half + 128].reshape(3, 128, 128)
            ancv[8 + 4 * half + k, tiles(chunk)] = ancv[2 * k + half, tiles(chunk)] + part
        copy = remote(
            ancv.at[8 + 4 * (1 - core) + k, tiles(chunk)], qr.at[k, tiles(chunk)],
            es.at[chunk, k], er.at[chunk, k], row, other,
        )
        copy.start()
        swaps[chunk, k] = copy

    def merged(chunk, k):
        swaps[chunk, k].wait_recv()
        ancv[16 + k, tiles(chunk)] = ancv[8 + 4 * core + k, tiles(chunk)] + qr[k, tiles(chunk)]

    def move(chunk, n, k, part, dst, dx):
        copy = remote(
            ancv.at[16 + k, tiles(chunk), part], dst, rs.at[chunk, n], rr.at[chunk, n], row, along(dx)
        )
        copy.start()
        moves[chunk, n] = copy

    def far(chunk):
        move(chunk, 0, 0, UPPER, d2r.at[chunk, 0], 1)
        move(chunk, 1, 0, LOWER, d2r.at[chunk, 1], -1)

    def near_up(chunk):
        move(chunk, 2, 1, LOWER, d1r.at[chunk, 0, :, LOWER], 1)

    def near_down(chunk):
        move(chunk, 3, 2, UPPER, d1r.at[chunk, 1, :, UPPER], -1)

    def passed(chunk):
        moves[chunk, 0].wait_recv()
        ancv[17, tiles(chunk), UPPER] += d2r[chunk, 0]
        move(chunk, 4, 1, UPPER, d1r.at[chunk, 0, :, UPPER], 1)
        moves[chunk, 1].wait_recv()
        ancv[18, tiles(chunk), LOWER] += d2r[chunk, 1]
        move(chunk, 5, 2, LOWER, d1r.at[chunk, 1, :, LOWER], -1)

    tile_copies = {}

    def finish(chunk):
        for n in (2, 3, 4, 5):
            moves[chunk, n].wait_recv()
        for t in range(3):
            total = -(ancv[19, 3 * chunk + t] + d1r[chunk, 0, t] + d1r[chunk, 1, t])
            co[chunk, 2 * t] = total[:64]
            co[chunk, 2 * t + 1] = total[64:]
        for t in range(16):
            slots[chunk, t] = co[chunk, table[SLOT + t]]
        for k, peer in enumerate(peers):
            copy = remote(slots.at[chunk, peer], inc.at[chunk, row], as_.at[chunk, k], ar.at[chunk, k], peer, col)
            copy.start()
            tile_copies[chunk, k] = copy
        inc[chunk, row] = slots[chunk, row]

    product(3, 0)
    columns(0, 0)
    columns(0, 1)
    merged(0, 0)
    far(0)
    columns(0, 2)
    merged(0, 1)
    near_up(0)
    columns(0, 3)
    merged(0, 2)
    near_down(0)
    product(3, 1)
    merged(0, 3)
    columns(1, 0)
    passed(0)
    columns(1, 1)
    merged(1, 0)
    far(1)
    columns(1, 2)
    merged(1, 1)
    near_up(1)
    columns(1, 3)
    merged(1, 2)
    near_down(1)
    merged(1, 3)
    hand_over(0)
    finish(0)
    passed(1)
    share(1)
    for m in range(8):
        s = pl.ds(128 * m, 128)
        lh[:, s], ll[:, s] = split(inv[s, :].T)
    finish(1)
    hand_over(1)
    spread_end(0)
    spread_end(1)

    for chunk in range(2):
        for k in range(15):
            mine = inc.at[chunk, origins[k]]
            remote(mine, mine, as_.at[chunk, k], ar.at[chunk, k], peers[k], col).wait_recv()
    for i in range(6):
        for half in range(2):
            tile = inc[half, table[FROM + i]]
            tile = jnp.where(jnp.full((64, 128), table[KEEP + i]) == 1, tile, 0.0)
            r = pl.ds(128 * i + 64 * half, 64)
            cov[r, :] = tile
            ch[r, :], cl[r, :] = split(tile)
    for m in range(4):
        rows = brx[pl.ds(4 * m, 4)].reshape(256, 768)
        part = dot3(*split(rows), ch[pl.ds(0, 768), :], cl[pl.ds(0, 768), :])
        for i in range(4):
            for h in range(2):
                place = rel(h, *ITEMS[4 * m + i])
                wp[place // 4, place % 4, h] = part[64 * i + 32 * h : 64 * i + 32 * h + 32]
    steps = {}

    def step_to(h, axis, d):
        return at(0, d) if axis == 0 else at(d, 0)

    def exchange(stage, h, d, axis, src, dst, mine):
        copy = remote(src, dst, bs.at[stage, h, d - 1], br.at[stage, h, d - 1], step_to(h, axis, d), col)
        copy.start()
        got = remote(mine, mine, bs.at[stage, h, d - 1], br.at[stage, h, d - 1], step_to(h, axis, d), col)
        steps[stage, h, d] = (copy, got)

    DS = (1, 3, 2)
    for d in DS:
        zd, yd = lax.rem(z + d, 4), lax.rem(y + d, 4)
        exchange(0, 0, d, 0, wp.at[:, zd, 0], w1.at[0, d - 1], w1.at[0, d - 1])
        exchange(0, 1, d, 1, wp.at[yd, :, 1], w1.at[1, d - 1], w1.at[1, d - 1])
    for h in both:
        value = wp[:, z, 0] if h == 0 else wp[y, :, 1]
        for d in DS:
            steps[0, h, d][1].wait_recv()
            value += w1[h, d - 1]
        s1[h] = value
        for d in DS:
            there = lax.rem((y if h == 0 else z) + d, 4)
            exchange(1, h, d, 1 - h, s1.at[h, there], w2.at[h, d - 1], w2.at[h, d - 1])
    for h in both:
        place = y if h == 0 else z
        here = pl.ds(pl.multiple_of(row * 64 + 32 * h, 32), 32)
        value = inv[here, pl.ds(pl.multiple_of(col * 128, 128), 128)]
        value = jnp.where(jnp.full((32, 128), table[TURN]) == 0, value, 0.0) - s1[h, place]
        for d in DS:
            steps[1, h, d][1].wait_recv()
            value -= w2[h, d - 1]
        g1[h, place] = value
        for d in DS:
            back = lax.rem(place + 4 - d, 4)
            exchange(2, h, d, 1 - h, g1.at[h, place], g1.at[h, place], g1.at[h, back])
    for h in both:
        for d in DS:
            steps[2, h, d][1].wait_recv()
        if h == 0:
            wall[:, z, 0] = g1[0]
        else:
            wall[y, :, 1] = g1[1]
        for d in DS:
            if h == 0:
                exchange(3, h, d, 0, g1.at[0], wall.at[:, z, 0], wall.at[:, lax.rem(z + 4 - d, 4), 0])
            else:
                exchange(3, h, d, 1, g1.at[1], wall.at[y, :, 1], wall.at[lax.rem(y + 4 - d, 4), :, 1])
    for h in both:
        for d in DS:
            steps[3, h, d][1].wait_recv()
    ch[...], cl[...] = split(wall[...].reshape(1024, 128))
    for m in range(4):
        r = pl.ds(256 * m, 256)
        cov_diag[r, :] = dot3(lh[r, :], ll[r, :], ch[...], cl[...])
    for copy in sends + swap_inv + list(swaps.values()) + list(moves.values()) + list(tile_copies.values()):
        copy.wait_send()
    for copy, _ in steps.values():
        copy.wait_send()
    spread_sent()


def shape(dims, dtype=F32):
    return jax.ShapeDtypeStruct(dims, dtype)


def shards(ancestor_inv, update_tiles, tile_slot, lower_below, diag_factor):
    vm = pltpu.VMEM
    dma = pltpu.SemaphoreType.DMA

    first, second, more = pl.pallas_call(
        tables,
        out_shape=[shape((64,), jnp.int32), shape((64,), jnp.int32), shape((1,), jnp.int32)],
        in_specs=[SMEM, SMEM],
        out_specs=[SMEM] * 3,
        scratch_shapes=[pltpu.SMEM((16,), jnp.int32)],
        name="tables",
    )(update_tiles, tile_slot)

    def call(table):
        return pl.pallas_call(
            work,
            out_shape=[shape((768, 128)), shape((1024, 128))],
            in_specs=[SMEM, ANY, ANY, ANY],
            out_specs=[VMEM, VMEM],
            scratch_shapes=[
                vm((24, 12, 128, 128), F32), vm((16, 64, 1536), F32), vm((768, 1536), BF16), vm((768, 1536), BF16),
                vm((1536, 256), BF16), vm((1536, 256), BF16), vm((768, 1024), BF16), vm((768, 1024), BF16),
                vm((4, 6, 128, 128), F32), vm((2, 2, 3, 64, 128), F32), vm((2, 2, 3, 128, 128), F32),
                vm((16, 64, 768), F32), vm((1024, 1024), F32), vm((1024, 1024), F32), vm((1024, 1024), BF16),
                vm((1024, 1024), BF16), vm((2, 6, 64, 128), F32), vm((2, 16, 64, 128), F32), vm((2, 16, 64, 128), F32),
                vm((4, 4, 2, 32, 128), F32), vm((2, 3, 4, 32, 128), F32), vm((2, 4, 32, 128), F32),
                vm((2, 3, 32, 128), F32), vm((2, 4, 32, 128), F32), vm((4, 4, 2, 32, 128), F32),
                vm((1024, 128), BF16), vm((1024, 128), BF16),
                dma((24,)), dma(()), dma(()), dma((40,)), dma((40,)), dma((16, 3)), dma((16,)), dma((2, 3)), dma((2, 3)), dma((2,)), dma((2,)),
                dma((2, 4)), dma((2, 4)), dma((2, 6)), dma((2, 6)), dma(()), dma(()), dma((2, 15)), dma((2, 15)),
                dma((4, 2, 3)), dma((4, 2, 3)),
            ],
            compiler_params=pltpu.CompilerParams(vmem_limit_bytes=LIMIT, collective_id=0, has_side_effects=True),
            name="work",
        )(table, ancestor_inv.reshape(12, 128, 3072), lower_below.T, diag_factor)

    cov_below, cov_diag = call(first)

    def again(cov_below, cov_diag):
        more_below, more_diag = call(second)
        return cov_below + more_below, cov_diag + more_diag

    return lax.cond(more[0] == 1, again, lambda a, b: (a, b), cov_below, cov_diag)


def solution(mesh):
    in_specs = (P("row", "col"), P(), P(), P("col", "row"), P())
    out_specs = (P("row", "col"), P(None, "col"))
    return jax.shard_map(shards, mesh=mesh, in_specs=in_specs, out_specs=out_specs, check_vma=False)
```

```python
import jax
import jax.numpy as jnp
from jax import lax
from jax.experimental import pallas as pl
from jax.experimental.pallas import tpu as pltpu
from jax.sharding import PartitionSpec as P

TILE = 128
ATILES = 192
UTILES = 96
JW = 1024
MESH = pl.DeviceIdType.MESH
F32, BF16 = jnp.float32, jnp.bfloat16
VMEM = pl.BlockSpec(memory_space=pltpu.VMEM)
SMEM = pl.BlockSpec(memory_space=pltpu.SMEM)
ANY = pl.BlockSpec(memory_space=pl.ANY)
LIMIT = 60 * 1024 * 1024
ROWS, COLS, SLOT, FROM, KEEP, TURN = 0, 8, 20, 36, 42, 48
FULL, LOW, HIGH = (0, 32), (0, 16), (16, 16)


def split(value):
    high = value.astype(BF16)
    return high, (value - high.astype(F32)).astype(BF16)


def dot3(ah, al, bh, bl):
    out = jnp.dot(ah, bh, preferred_element_type=F32)
    out += jnp.dot(ah, bl, preferred_element_type=F32)
    return out + jnp.dot(al, bh, preferred_element_type=F32)


def remote(src, dst, send, recv, row, col):
    return pltpu.make_async_remote_copy(
        src_ref=src, dst_ref=dst, send_sem=send, recv_sem=recv, device_id=(row, col), device_id_type=MESH
    )


def greet(peers, more, far, extra):
    barrier = pltpu.get_barrier_semaphore()
    for peer in peers:
        pl.semaphore_signal(barrier, inc=1, device_id=peer, device_id_type=MESH)

    @pl.when(more)
    def _():
        pl.semaphore_signal(barrier, inc=1, device_id=far, device_id_type=MESH)

    pl.semaphore_wait(barrier, len(peers) + extra)


def tables(upd, slots, first, second, more, counts):
    row, col = lax.axis_index("row"), lax.axis_index("col")
    more[0] = 0
    for i in range(16):
        counts[i] = 0
    for turn, table in enumerate((first, second)):
        for i in range(48):
            table[i] = 0
        for k in range(12):
            table[COLS + k] = upd[12 * col + k] - 24 * col
        table[TURN] = turn

    def visit(u, carry):
        slot = slots[upd[u]]
        owner = slot // 12
        seen = counts[owner]
        counts[owner] = seen + 1
        target = u // 6

        @pl.when(seen >= 6)
        def _():
            more[0] = 1

        @pl.when(owner == row)
        def _():
            for turn, table in enumerate((first, second)):

                @pl.when(seen // 6 == turn)
                def _():
                    table[ROWS + seen - 6 * turn] = slot - 12 * row
                    table[SLOT + target] = seen - 6 * turn

        @pl.when(target == row)
        def _():
            for turn, table in enumerate((first, second)):
                table[FROM + u - 6 * row] = owner
                table[KEEP + u - 6 * row] = jnp.where(seen // 6 == turn, 1, 0)

        return carry

    lax.fori_loop(0, UTILES, visit, 0)


ITEMS = (
    (0, 0), (0, -1), (0, 1), (-1, 0), (1, 0), (0, 2), (2, 0), (-1, -1),
    (1, -1), (-1, 1), (1, 1), (-1, 2), (1, 2), (2, -1), (2, 1), (2, 2),
)


def work(
    table, anc, lbt, diag, cov, cov_diag,
    ancv, bg, sh, sl, bh, bl, ph, pq, qr, d2r, d1r, brx, dg, inv, lh, ll,
    co, slots, inc, wp, w1, s1, w2, g1, wall, ch, cl,
    anc_sem, own_sem, dg_sem, gs, gr, xs, sr, ss, sg, ps, pr, es, er, rs, rr, is_, ir, as_, ar, bs, br,
):
    row, col = lax.axis_index("row"), lax.axis_index("col")
    y, z, x, core = row // 4, row % 4, col // 2, col % 2
    other = 2 * x + 1 - core

    def at(dy, dz):
        return 4 * lax.rem(y + dy + 4, 4) + lax.rem(z + dz + 4, 4)

    def along(dx):
        return 2 * lax.rem(x + dx + 4, 4) + core

    own = pltpu.make_async_copy(lbt, bg.at[row], own_sem)
    own.start()
    dg_load = pltpu.make_async_copy(diag, dg, dg_sem)
    dg_load.start()
    loads = [
        pltpu.make_async_copy(anc.at[:, :, pl.ds(128 * t, 128)], ancv.at[t], anc_sem.at[t])
        for t in range(24)
    ]
    for load in loads:
        load.start()
    peers = [lax.rem(row + d, 16) for d in range(1, 16)]
    origins = [lax.rem(row + 16 - d, 16) for d in range(1, 16)]
    parity = row % 2
    root_x, root_core = row // 4, (row // 2) % 2
    dist = lax.rem(x - root_x + 4, 4)
    ring = core == root_core
    opposite = jnp.where(ring & (dist != 2), 1, 0)
    greet(
        [(peer, col) for peer in peers] + [(row, along(1)), (row, along(-1)), (row, other)],
        ring & (dist != 0), (row, along(2)), opposite,
    )
    own.wait()

    def rel(h, a, b):
        return at(a, b) if h == 0 else at(b, a)

    ids = {}
    sends = []

    def gather(name, h, src, rows, step, recv_src):
        k = ids.setdefault((h, name), len(ids))
        part = pl.ds(32 * h + rows[0], rows[1])
        view = bg.at[rel(h, *src), part]
        copy = remote(view, view, gs.at[k], gr.at[k], rel(h, *step), col)
        copy.start()
        mine = bg.at[rel(h, *recv_src), part]
        got = remote(mine, mine, gs.at[k], gr.at[k], rel(h, *step), col)
        sends.append(copy)
        return got

    arr = {}

    def first_phase(h):
        arr[h, 0, -1] = [gather("f+", h, (0, 0), FULL, (0, 1), (0, -1))]
        arr[h, 0, 1] = [gather("f-", h, (0, 0), FULL, (0, -1), (0, 1))]

    def first_forward(h):
        arr[h, 0, 2] = [
            gather("ff+", h, (0, -1), LOW, (0, 1), (0, -2)),
            gather("ff-", h, (0, 1), HIGH, (0, -1), (0, 2)),
        ]

    def second_phase(h, q):
        arr[h, -1, q] = [gather(("s+", q), h, (0, q), FULL, (1, 0), (-1, q))]
        arr[h, 1, q] = [gather(("s-", q), h, (0, q), FULL, (-1, 0), (1, q))]

    def second_forward(h, q):
        arr[h, 2, q] = [
            gather(("sf+", q), h, (-1, q), LOW, (1, 0), (-2, q)),
            gather(("sf-", q), h, (1, q), HIGH, (-1, 0), (2, q)),
        ]

    def wait(h, a, b):
        for got in arr[h, a, b]:
            got.wait_recv()

    def quarter(d):
        return pl.ds(pl.multiple_of(16 * d, 16), 16)

    def chip(d):
        return 2 * lax.rem(root_x + d, 4) + root_core

    def scatter_copy(i, d):
        view = brx.at[i, quarter(d)]
        return remote(view, view, xs.at[i, d - 1], sr.at[i], row, chip(d))

    def scatter(i):
        @pl.when(ring & (dist == 0))
        def _():
            lanes = pl.ds(pl.multiple_of(768 * parity, 768), 768)
            for h in range(2):
                brx[i, pl.ds(32 * h, 32), :] = bg[rel(h, *ITEMS[i]), pl.ds(32 * h, 32), lanes]
            for d in (1, 2, 3):
                scatter_copy(i, d).start()

    def batch(b):
        return pl.ds(8 * b, 8)

    def share_copy(b, e):
        view = brx.at[batch(b), quarter(dist)]
        return remote(view, view, ss.at[b, e - 1], sg.at[b, e - 1], row, along(e))

    def share(b):
        for i in range(8 * b, 8 * b + 8):

            @pl.when(ring & (dist != 0))
            def _():
                view = brx.at[i, quarter(dist)]
                remote(view, view, xs.at[i, 0], sr.at[i], row, along(1)).wait_recv()

        for e in (1, 3, 2):

            @pl.when(ring & (lax.rem(dist + e, 4) != 0))
            def _():
                share_copy(b, e).start()

    def partner_copy(b):
        view = brx.at[batch(b)]
        return remote(view, view, ps.at[b], pr.at[b], row, other)

    def hand_over(b):
        @pl.when(ring & (dist != 0))
        def _():
            for e in (1, 2, 3):
                view = brx.at[batch(b), quarter(lax.rem(dist - e + 4, 4))]
                remote(view, view, ss.at[b, e - 1], sg.at[b, e - 1], row, along(e)).wait_recv()

        @pl.when(ring)
        def _():
            partner_copy(b).start()

    def spread_end(b):
        @pl.when(jnp.logical_not(ring))
        def _():
            partner_copy(b).wait_recv()

    def spread_sent():
        for b in range(2):

            @pl.when(ring)
            def _():
                partner_copy(b).wait_send()

            for e in (1, 2, 3):

                @pl.when(ring & (lax.rem(dist + e, 4) != 0))
                def _():
                    share_copy(b, e).wait_send()

        @pl.when(ring & (dist == 0))
        def _():
            for i in range(16):
                for d in (1, 2, 3):
                    scatter_copy(i, d).wait_send()

    def spread_step(i):
        scatter(i)

    def extract(j, carry):
        for k in range(12):
            high, low = split(ancv[table[COLS + k], table[ROWS + j]])
            c = pl.ds(128 * k, 128)
            for half in range(2):
                dst = pl.ds(pl.multiple_of(384 * half + j * 64, 64), 64)
                sh[dst, c] = high[64 * half : 64 * half + 64]
                sl[dst, c] = low[64 * half : 64 * half + 64]
        return carry

    base = pl.multiple_of(512 * core, 512)
    i256 = lax.broadcasted_iota(jnp.int32, (256, 256), 0)
    j256 = lax.broadcasted_iota(jnp.int32, (256, 256), 1)

    def sub(b, size):
        return pl.ds(pl.multiple_of(base + size * b, size), size)

    def inverse_start():
        dg_load.wait()
        inv[pl.ds(0, 512), pl.ds(512, 512)] = jnp.zeros((512, 512), F32)
        inv[sub(0, 256), sub(1, 256)] = jnp.zeros((256, 256), F32)
        for b in range(2):
            s = sub(b, 256)
            inv[s, s] = jnp.where(i256 == j256, 1.0 / dg[s, s], 0.0)

    def inverse_levels(first, last):
        def level(n, carry):
            bi, bj = lax.shift_right_logical(i256, n), lax.shift_right_logical(j256, n)
            mask = (bi == bj + 1) & ((bi & 1) == 1)
            for b in range(2):
                s = sub(b, 256)
                value = inv[s, s]
                part = split(value)
                inner = dot3(*split(jnp.where(mask, dg[s, s], 0.0)), *part)
                inv[s, s] = value - dot3(*part, *split(inner))
            return carry

        lax.fori_loop(first, last, level, 0)

    swap_inv = []

    def inverse_512():
        top, low = sub(0, 256), sub(1, 256)
        inner = dot3(*split(dg[low, top]), *split(inv[top, top]))
        inv[low, top] = -dot3(*split(inv[low, low]), *split(inner))
        block = inv.at[pl.ds(base, 512), pl.ds(base, 512)]
        copy = remote(block, block, is_, ir, row, other)
        copy.start()
        swap_inv.append(copy)

    def inverse_1024():
        there = pl.ds(pl.multiple_of(512 - base, 512), 512)
        block = inv.at[there, there]
        remote(block, block, is_, ir, row, other).wait_recv()
        top, low = pl.ds(0, 512), pl.ds(512, 512)
        xh, xl = split(inv[top, top])
        for m in range(2):
            r = pl.ds(512 + 256 * m, 256)
            inner = dot3(*split(dg[r, top]), xh, xl)
            dg[r, top] = inner
        ih, il = split(dg[low, top])
        for m in range(2):
            r = pl.ds(512 + 256 * m, 256)
            inv[r, top] = -dot3(*split(inv[r, low]), ih, il)

    def inverse_rows():
        for i, item in enumerate(ITEMS):
            for h in range(2):
                src = pl.ds(pl.multiple_of(64 * rel(h, *item) + 32 * h, 32), 32)
                dst = pl.ds(64 * i + 32 * h, 32)
                lh[dst, :], ll[dst, :] = split(inv[src, :])

    def build(g):
        for p in range(2):
            for k in range(12):
                lanes = pl.ds(128 * k, 128)
                rows = [
                    bg[rel(h, *ITEMS[4 * g + 2 * p + i]), pl.ds(32 * h, 32), lanes]
                    for i in range(2)
                    for h in range(2)
                ]
                c = pl.ds(128 * p, 128)
                bh[lanes, c], bl[lanes, c] = split(jnp.concatenate(rows, axis=0).T)

    def product(g, chunk):
        r = pl.ds(384 * chunk, 384)
        c = pl.ds(256 * g, 256)
        ph[r, c], pq[r, c] = split(dot3(sh[r, :], sl[r, :], bh[...], bl[...]))

    def group(g):
        build(g)
        for chunk in range(2):
            product(g, chunk)

    def block(dx):
        return pl.ds(pl.multiple_of(256 * lax.rem(x + dx + 4, 4), 256), 256)

    DX = (2, 1, -1, 0)
    EARLY, LATE = pl.ds(0, 768), pl.ds(768, 256)

    def early_columns(k):
        c = block(DX[k])
        for chunk in range(2):
            r = pl.ds(384 * chunk, 384)
            acc = dot3(ph[r, EARLY], pq[r, EARLY], lh[EARLY, c], ll[EARLY, c])
            for half in range(2):
                ancv[2 * k + half, pl.ds(3 * chunk, 3)] = acc[:, 128 * half : 128 * half + 128].reshape(3, 128, 128)

    both = (0, 1)
    for h in both:
        first_phase(h)
    for h in both:
        second_phase(h, 0)
    spread_step(0)
    for q in (-1, 1):
        for h in both:
            wait(h, 0, q)
        if q == 1:
            for h in both:
                first_forward(h)
        for h in both:
            second_phase(h, q)
    spread_step(1)
    spread_step(2)
    inverse_start()
    inverse_levels(0, 4)
    for h in both:
        wait(h, -1, 0)
        wait(h, 1, 0)
        second_forward(h, 0)
    spread_step(3)
    spread_step(4)
    for load in loads:
        load.wait()
    lax.fori_loop(0, 6, extract, 0)
    for h in both:
        wait(h, 0, 2)
        second_phase(h, 2)
    spread_step(5)
    inverse_levels(4, 8)
    inverse_512()
    for h in both:
        wait(h, 2, 0)
    spread_step(6)
    for q, i in ((-1, 7), (1, 9)):
        for h in both:
            wait(h, -1, q)
            wait(h, 1, q)
            second_forward(h, q)
        spread_step(i)
        spread_step(i + 1)
        group(0 if q == -1 else 1)
    inverse_1024()
    inverse_rows()
    for h in both:
        wait(h, -1, 2)
        wait(h, 1, 2)
        second_forward(h, 2)
    spread_step(11)
    spread_step(12)
    group(2)
    share(0)
    for h in both:
        wait(h, 2, -1)
        wait(h, 2, 1)
    spread_step(13)
    spread_step(14)
    for k in range(4):
        early_columns(k)
    for h in both:
        wait(h, 2, 2)
    spread_step(15)
    build(3)

    UPPER, LOWER = pl.ds(0, 64), pl.ds(64, 64)
    swaps, moves = {}, {}

    def tiles(chunk):
        return pl.ds(3 * chunk, 3)

    def columns(chunk, k):
        r = pl.ds(384 * chunk, 384)
        c = block(DX[k])
        acc = dot3(ph[r, LATE], pq[r, LATE], lh[LATE, c], ll[LATE, c])
        for half in range(2):
            part = acc[:, 128 * half : 128 * half + 128].reshape(3, 128, 128)
            ancv[8 + 4 * half + k, tiles(chunk)] = ancv[2 * k + half, tiles(chunk)] + part
        copy = remote(
            ancv.at[8 + 4 * (1 - core) + k, tiles(chunk)], qr.at[k, tiles(chunk)],
            es.at[chunk, k], er.at[chunk, k], row, other,
        )
        copy.start()
        swaps[chunk, k] = copy

    def merged(chunk, k):
        swaps[chunk, k].wait_recv()
        ancv[16 + k, tiles(chunk)] = ancv[8 + 4 * core + k, tiles(chunk)] + qr[k, tiles(chunk)]

    def move(chunk, n, k, part, dst, dx):
        copy = remote(
            ancv.at[16 + k, tiles(chunk), part], dst, rs.at[chunk, n], rr.at[chunk, n], row, along(dx)
        )
        copy.start()
        moves[chunk, n] = copy

    def far(chunk):
        move(chunk, 0, 0, UPPER, d2r.at[chunk, 0], 1)
        move(chunk, 1, 0, LOWER, d2r.at[chunk, 1], -1)

    def near_up(chunk):
        move(chunk, 2, 1, LOWER, d1r.at[chunk, 0, :, LOWER], 1)

    def near_down(chunk):
        move(chunk, 3, 2, UPPER, d1r.at[chunk, 1, :, UPPER], -1)

    def passed(chunk):
        moves[chunk, 0].wait_recv()
        ancv[17, tiles(chunk), UPPER] += d2r[chunk, 0]
        move(chunk, 4, 1, UPPER, d1r.at[chunk, 0, :, UPPER], 1)
        moves[chunk, 1].wait_recv()
        ancv[18, tiles(chunk), LOWER] += d2r[chunk, 1]
        move(chunk, 5, 2, LOWER, d1r.at[chunk, 1, :, LOWER], -1)

    tile_copies = {}

    def finish(chunk):
        for n in (2, 3, 4, 5):
            moves[chunk, n].wait_recv()
        for t in range(3):
            total = -(ancv[19, 3 * chunk + t] + d1r[chunk, 0, t] + d1r[chunk, 1, t])
            co[chunk, 2 * t] = total[:64]
            co[chunk, 2 * t + 1] = total[64:]
        for t in range(16):
            slots[chunk, t] = co[chunk, table[SLOT + t]]
        for k, peer in enumerate(peers):
            copy = remote(slots.at[chunk, peer], inc.at[chunk, row], as_.at[chunk, k], ar.at[chunk, k], peer, col)
            copy.start()
            tile_copies[chunk, k] = copy
        inc[chunk, row] = slots[chunk, row]

    product(3, 0)
    columns(0, 0)
    columns(0, 1)
    merged(0, 0)
    far(0)
    columns(0, 2)
    merged(0, 1)
    near_up(0)
    columns(0, 3)
    merged(0, 2)
    near_down(0)
    product(3, 1)
    merged(0, 3)
    columns(1, 0)
    passed(0)
    columns(1, 1)
    merged(1, 0)
    far(1)
    columns(1, 2)
    merged(1, 1)
    near_up(1)
    columns(1, 3)
    merged(1, 2)
    near_down(1)
    merged(1, 3)
    finish(0)
    passed(1)
    share(1)
    hand_over(0)
    for m in range(8):
        s = pl.ds(128 * m, 128)
        lh[:, s], ll[:, s] = split(inv[s, :].T)
    finish(1)
    hand_over(1)
    spread_end(0)
    spread_end(1)

    for chunk in range(2):
        for k in range(15):
            mine = inc.at[chunk, origins[k]]
            remote(mine, mine, as_.at[chunk, k], ar.at[chunk, k], peers[k], col).wait_recv()
    for i in range(6):
        for half in range(2):
            tile = inc[half, table[FROM + i]]
            tile = jnp.where(jnp.full((64, 128), table[KEEP + i]) == 1, tile, 0.0)
            r = pl.ds(128 * i + 64 * half, 64)
            cov[r, :] = tile
            ch[r, :], cl[r, :] = split(tile)
    for m in range(4):
        rows = brx[pl.ds(4 * m, 4)].reshape(256, 768)
        part = dot3(*split(rows), ch[pl.ds(0, 768), :], cl[pl.ds(0, 768), :])
        for i in range(4):
            for h in range(2):
                place = rel(h, *ITEMS[4 * m + i])
                wp[place // 4, place % 4, h] = part[64 * i + 32 * h : 64 * i + 32 * h + 32]
    steps = {}

    def step_to(h, axis, d):
        return at(0, d) if axis == 0 else at(d, 0)

    def exchange(stage, h, d, axis, src, dst, mine):
        copy = remote(src, dst, bs.at[stage, h, d - 1], br.at[stage, h, d - 1], step_to(h, axis, d), col)
        copy.start()
        got = remote(mine, mine, bs.at[stage, h, d - 1], br.at[stage, h, d - 1], step_to(h, axis, d), col)
        steps[stage, h, d] = (copy, got)

    DS = (1, 3, 2)
    for d in DS:
        zd, yd = lax.rem(z + d, 4), lax.rem(y + d, 4)
        exchange(0, 0, d, 0, wp.at[:, zd, 0], w1.at[0, d - 1], w1.at[0, d - 1])
        exchange(0, 1, d, 1, wp.at[yd, :, 1], w1.at[1, d - 1], w1.at[1, d - 1])
    for h in both:
        value = wp[:, z, 0] if h == 0 else wp[y, :, 1]
        for d in DS:
            steps[0, h, d][1].wait_recv()
            value += w1[h, d - 1]
        s1[h] = value
        for d in DS:
            there = lax.rem((y if h == 0 else z) + d, 4)
            exchange(1, h, d, 1 - h, s1.at[h, there], w2.at[h, d - 1], w2.at[h, d - 1])
    for h in both:
        place = y if h == 0 else z
        here = pl.ds(pl.multiple_of(row * 64 + 32 * h, 32), 32)
        value = inv[here, pl.ds(pl.multiple_of(col * 128, 128), 128)]
        value = jnp.where(jnp.full((32, 128), table[TURN]) == 0, value, 0.0) - s1[h, place]
        for d in DS:
            steps[1, h, d][1].wait_recv()
            value -= w2[h, d - 1]
        g1[h, place] = value
        for d in DS:
            back = lax.rem(place + 4 - d, 4)
            exchange(2, h, d, 1 - h, g1.at[h, place], g1.at[h, place], g1.at[h, back])
    for h in both:
        for d in DS:
            steps[2, h, d][1].wait_recv()
        if h == 0:
            wall[:, z, 0] = g1[0]
        else:
            wall[y, :, 1] = g1[1]
        for d in DS:
            if h == 0:
                exchange(3, h, d, 0, g1.at[0], wall.at[:, z, 0], wall.at[:, lax.rem(z + 4 - d, 4), 0])
            else:
                exchange(3, h, d, 1, g1.at[1], wall.at[y, :, 1], wall.at[lax.rem(y + 4 - d, 4), :, 1])
    for h in both:
        for d in DS:
            steps[3, h, d][1].wait_recv()
    ch[...], cl[...] = split(wall[...].reshape(1024, 128))
    for m in range(4):
        r = pl.ds(256 * m, 256)
        cov_diag[r, :] = dot3(lh[r, :], ll[r, :], ch[...], cl[...])
    for copy in sends + swap_inv + list(swaps.values()) + list(moves.values()) + list(tile_copies.values()):
        copy.wait_send()
    for copy, _ in steps.values():
        copy.wait_send()
    spread_sent()


def shape(dims, dtype=F32):
    return jax.ShapeDtypeStruct(dims, dtype)


def shards(ancestor_inv, update_tiles, tile_slot, lower_below, diag_factor):
    vm = pltpu.VMEM
    dma = pltpu.SemaphoreType.DMA

    first, second, more = pl.pallas_call(
        tables,
        out_shape=[shape((64,), jnp.int32), shape((64,), jnp.int32), shape((1,), jnp.int32)],
        in_specs=[SMEM, SMEM],
        out_specs=[SMEM] * 3,
        scratch_shapes=[pltpu.SMEM((16,), jnp.int32)],
        name="tables",
    )(update_tiles, tile_slot)

    def call(table):
        return pl.pallas_call(
            work,
            out_shape=[shape((768, 128)), shape((1024, 128))],
            in_specs=[SMEM, ANY, ANY, ANY],
            out_specs=[VMEM, VMEM],
            scratch_shapes=[
                vm((24, 12, 128, 128), F32), vm((16, 64, 1536), F32), vm((768, 1536), BF16), vm((768, 1536), BF16),
                vm((1536, 256), BF16), vm((1536, 256), BF16), vm((768, 1024), BF16), vm((768, 1024), BF16),
                vm((4, 6, 128, 128), F32), vm((2, 2, 3, 64, 128), F32), vm((2, 2, 3, 128, 128), F32),
                vm((16, 64, 768), F32), vm((1024, 1024), F32), vm((1024, 1024), F32), vm((1024, 1024), BF16),
                vm((1024, 1024), BF16), vm((2, 6, 64, 128), F32), vm((2, 16, 64, 128), F32), vm((2, 16, 64, 128), F32),
                vm((4, 4, 2, 32, 128), F32), vm((2, 3, 4, 32, 128), F32), vm((2, 4, 32, 128), F32),
                vm((2, 3, 32, 128), F32), vm((2, 4, 32, 128), F32), vm((4, 4, 2, 32, 128), F32),
                vm((1024, 128), BF16), vm((1024, 128), BF16),
                dma((24,)), dma(()), dma(()), dma((40,)), dma((40,)), dma((16, 3)), dma((16,)), dma((2, 3)), dma((2, 3)), dma((2,)), dma((2,)),
                dma((2, 4)), dma((2, 4)), dma((2, 6)), dma((2, 6)), dma(()), dma(()), dma((2, 15)), dma((2, 15)),
                dma((4, 2, 3)), dma((4, 2, 3)),
            ],
            compiler_params=pltpu.CompilerParams(vmem_limit_bytes=LIMIT, collective_id=0, has_side_effects=True),
            name="work",
        )(table, ancestor_inv.reshape(12, 128, 3072), lower_below.T, diag_factor)

    cov_below, cov_diag = call(first)

    def again(cov_below, cov_diag):
        more_below, more_diag = call(second)
        return cov_below + more_below, cov_diag + more_diag

    return lax.cond(more[0] == 1, again, lambda a, b: (a, b), cov_below, cov_diag)


def solution(mesh):
    in_specs = (P("row", "col"), P(), P(), P("col", "row"), P())
    out_specs = (P("row", "col"), P(None, "col"))
    return jax.shard_map(shards, mesh=mesh, in_specs=in_specs, out_specs=out_specs, check_vma=False)
```
